256 devices in a mesh: seq: 64 (over z, x, core), tp: 4 (over y).
Axes of the slice: x: 4, y: 4, z: 8, core: 2. Of those that a mesh axis runs over, the one named last changes fastest.
Arguments:
- prefix: bfloat16 [16384, 2048], P('seq', 'tp'), may hold values from -48 to 48
- latent_in: bfloat16 [1024, 2048], P('seq', 'tp'), may hold values from -48 to 48
- latent_pos: int32 [1024], replicated, may hold values from 4096 to 16383, as said below
- w_query: bfloat16 [2048, 2048], P(None, 'tp'), may hold values from -0.375 to 0.375
- w_keyval: bfloat16 [2, 2048, 2048], P(None, None, 'tp'), may hold values from -0.125 to 0.125
- w_cross_out: bfloat16 [2048, 2048], P('tp'), may hold values from -0.125 to 0.125
- attn_gain: float32 [2048], replicated, may hold values from 0.1 to 1.9
- w_self_qkv: bfloat16 [3, 2048, 2048], P(None, 'seq', 'tp'), may hold values from -0.91855865 to 0.91855865
- w_self_out: bfloat16 [2048, 2048], P('tp', 'seq'), may hold values from -0.125 to 0.125
- mlp_gain: float32 [2048], replicated, may hold values from 0.1 to 1.9
- w_gate_up: bfloat16 [2, 2048, 4096], P(None, 'seq', 'tp'), may hold values from -0.125 to 0.125
- w_down: bfloat16 [4096, 2048], P('tp', 'seq'), may hold values from -0.09375 to 0.09375
Outputs:
- latent_out: bfloat16 [1024, 2048], P('seq', 'tp')
The draws below stay inside these ranges and needn't reach their ends.
Inputs may be any that keep to these rules, and one draw needn't show every extreme that they name: `latent_pos`: strictly increasing; the first is 4096 and the last is 16383.
All inputs are finite; a program needn't handle non-finite values.
Results may differ from the reference program's by a relative error of at most 0.02895.
The reference program's roundings to bfloat16 on the way (of `queries`, `cross_context`, `first`, `normed`, `self_context`, `second`, `normed_mlp` and `hidden`) count: a program that leaves them out, or rounds other values in their place, can miss the bound.
Values may be sent and summed in bfloat16 or wider, within the bound.
No kernel may reach another device: no remote copies, remote signals or barrier semaphores. Data moves between devices by JAX's collectives and lax.ppermute only.
A program may use at most 64 MiB of HBM per device.

```python
import jax
import jax.numpy as jnp
from jax import lax

D = 2048
HEADS = 16
HD = 128
FF = 4096
LAT = 1024
PREFIX = 16384


def scaled_rows(key, count, width):
    key_values = jax.random.fold_in(key, 1)
    entries = jax.random.truncated_normal(key_values, -6.0, 6.0, (count, width), jnp.float32)
    return entries


def draw_prefix(key, part):
    key = jax.random.fold_in(key, 11)
    return scaled_rows(key, PREFIX, D).astype(jnp.bfloat16)


def draw_latent_in(key, part):
    key = jax.random.fold_in(key, 12)
    return scaled_rows(key, LAT, D).astype(jnp.bfloat16)


def draw_latent_pos(key, part):
    key = jax.random.fold_in(key, 13)
    span = PREFIX - PREFIX // 4
    inner = jax.random.permutation(key, span - 2)[:LAT - 2] + 1
    inner = jnp.sort(inner).astype(jnp.int32)
    first_one = jnp.zeros((1,), jnp.int32)
    last_one = jnp.full((1,), span - 1, jnp.int32)
    return (jnp.concatenate([first_one, inner, last_one]) + (PREFIX - span)).astype(jnp.int32)


def draw_w_self_qkv(key, part):
    key = jax.random.fold_in(key, 14)
    key_base = jax.random.fold_in(key, 0)
    base = jax.random.truncated_normal(key_base, -6.0, 6.0, (3, D, D), jnp.float32) * (3.0 / D) ** 0.5
    return base.astype(jnp.bfloat16)


def level_of(own_key, shape, pieces, least, largest):
    factor_of = 1.0
    for dim, blocks in pieces:
        steps = jax.random.uniform(jax.random.fold_in(jax.random.fold_in(own_key, 6), dim), (blocks,), jnp.float32, least / len(pieces), largest / len(pieces))
        factor_of = factor_of * jnp.repeat(jnp.exp(steps), shape[dim] // blocks).reshape((-1,) + (1,) * (len(shape) - 1 - dim))
    return factor_of


def scatter_about(rng, shape, scale, most, pieces=(), kind=jnp.bfloat16):
    array = scale * jax.random.normal(rng, shape, jnp.float32)
    if pieces:
        array = array * level_of(rng, shape, pieces, -0.22, 0.18)
    return jnp.clip(array, -most, most).astype(kind)


def setup_inputs(seed: int = 0) -> dict:
    streams_of = jax.random.split(jax.random.key(seed), 13)
    return {
        "prefix": draw_prefix(jax.random.fold_in(streams_of[12], 71), 0),
        "latent_in": draw_latent_in(jax.random.fold_in(streams_of[12], 71), 0),
        "latent_pos": draw_latent_pos(jax.random.fold_in(streams_of[12], 71), 0),
        "w_query": scatter_about(streams_of[3], (D, D), (D // 8) ** -0.5, 0.375, ((1, 4),)),
        "w_keyval": scatter_about(streams_of[4], (2, D, D), D ** -0.5, 0.125, ((2, 4),)),
        "w_cross_out": scatter_about(streams_of[5], (D, D), D ** -0.5, 0.125, ((0, 4),)),
        "attn_gain": jnp.clip(1.0 + 0.18 * jax.random.normal(streams_of[6], (D,), jnp.float32), 0.1, 1.9),
        "w_self_qkv": draw_w_self_qkv(jax.random.fold_in(streams_of[12], 71), 0),
        "w_self_out": scatter_about(streams_of[8], (D, D), D ** -0.5, 0.125, ((0, 4), (1, 64))),
        "mlp_gain": jnp.clip(1.0 + 0.18 * jax.random.normal(streams_of[9], (D,), jnp.float32), 0.1, 1.9),
        "w_gate_up": scatter_about(streams_of[10], (2, D, FF), D ** -0.5, 0.125, ((1, 64), (2, 4))),
        "w_down": scatter_about(streams_of[11], (FF, D), FF ** -0.5, 0.09375, ((0, 4), (1, 64))),
    }


NEG = -1e+30

def normalize(x, gain):
    x = x.astype(jnp.float32)
    scale = lax.rsqrt(lax.optimization_barrier(jnp.mean(x * x, axis=-1, keepdims=True)) + 1e-05)
    return (x * scale * gain.astype(jnp.float32)).astype(jnp.bfloat16)

def heads_first(x, count):
    return x.reshape(count, HEADS, HD).transpose(1, 0, 2)

def weighted_sum(weights, values):
    high = lax.optimization_barrier(weights.astype(jnp.bfloat16))
    low = (weights - high.astype(jnp.float32)).astype(jnp.bfloat16)
    return jnp.dot(high, values, preferred_element_type=jnp.float32) + jnp.dot(low, values, preferred_element_type=jnp.float32)

def reference(prefix, latent_in, latent_pos, w_query, w_keyval, w_cross_out, attn_gain, w_self_qkv, w_self_out, mlp_gain, w_gate_up, w_down):
    keys = jnp.dot(prefix, w_keyval[0], preferred_element_type=jnp.float32).astype(jnp.bfloat16)
    values = jnp.dot(prefix, w_keyval[1], preferred_element_type=jnp.float32).astype(jnp.bfloat16)
    queries = jnp.dot(latent_in, w_query, preferred_element_type=jnp.float32).astype(jnp.bfloat16)
    scale = HD ** (-0.5)
    visible = jnp.arange(PREFIX, dtype=jnp.int32)[None, :] <= latent_pos[:, None]

    def cross_head(triple):
        qhead, khead, vhead = triple
        scores = jnp.dot(qhead, khead.T, preferred_element_type=jnp.float32) * scale
        scores = jnp.where(visible, scores, NEG)
        peak = lax.optimization_barrier(jnp.max(scores, axis=1, keepdims=True))
        weights = jnp.where(visible, jnp.exp(scores - peak), 0.0)
        total = lax.optimization_barrier(jnp.sum(weights, axis=1, keepdims=True))
        summed = weighted_sum(weights, vhead)
        return summed / total
    cross = lax.map(cross_head, (heads_first(queries, LAT), heads_first(keys, PREFIX), heads_first(values, PREFIX)))
    cross_context = cross.transpose(1, 0, 2).reshape(LAT, D).astype(jnp.bfloat16)
    first = (latent_in.astype(jnp.float32) + jnp.dot(cross_context, w_cross_out, preferred_element_type=jnp.float32)).astype(jnp.bfloat16)
    normed = normalize(first, attn_gain)
    qkv = jnp.einsum('ld,cde->cle', normed.astype(jnp.float32), w_self_qkv.astype(jnp.float32)).astype(jnp.bfloat16)
    causal = jnp.arange(LAT, dtype=jnp.int32)[None, :] <= jnp.arange(LAT, dtype=jnp.int32)[:, None]

    def self_head(triple):
        qhead, khead, vhead = triple
        scores = jnp.dot(qhead, khead.T, preferred_element_type=jnp.float32) * scale
        scores = jnp.where(causal, scores, NEG)
        peak = lax.optimization_barrier(jnp.max(scores, axis=1, keepdims=True))
        weights = jnp.where(causal, jnp.exp(scores - peak), 0.0)
        total = lax.optimization_barrier(jnp.sum(weights, axis=1, keepdims=True))
        summed = weighted_sum(weights, vhead)
        return summed / total
    attended = lax.map(self_head, (heads_first(qkv[0], LAT), heads_first(qkv[1], LAT), heads_first(qkv[2], LAT)))
    self_context = attended.transpose(1, 0, 2).reshape(LAT, D).astype(jnp.bfloat16)
    second = (first.astype(jnp.float32) + jnp.dot(self_context, w_self_out, preferred_element_type=jnp.float32)).astype(jnp.bfloat16)
    normed_mlp = normalize(second, mlp_gain)
    gate = jnp.dot(normed_mlp, w_gate_up[0], preferred_element_type=jnp.float32)
    upward = jnp.dot(normed_mlp, w_gate_up[1], preferred_element_type=jnp.float32)
    hidden = (jax.nn.silu(gate) * upward).astype(jnp.bfloat16)
    latent_out = (second.astype(jnp.float32) + jnp.dot(hidden, w_down, preferred_element_type=jnp.float32)).astype(jnp.bfloat16)
    return latent_out
```

```python
import jax
import jax.numpy as jnp
from jax import lax
from jax.experimental import pallas as pl
from jax.experimental.pallas import tpu as pltpu
from jax.sharding import Mesh
from jax.sharding import PartitionSpec as P

HD = 128
NEG = -1e30
EPS = 1e-05
SCALE = HD ** (-0.5)
TP = 4
CORES = 2
LANES = 128
ZX = ("z", "x")
SEQ = ("z", "x", "core")
BF16 = jnp.bfloat16
F32 = jnp.float32
NT = (((1,), (1,)), ((), ()))
TN = (((0,), (0,)), ((), ()))


def shifted(x, axis, shift, count):
    return lax.ppermute(x, axis, [(i, (i + shift) % count) for i in range(count)])


def everyone(x):
    return [x] + [shifted(x, "tp", k, TP) for k in range(1, TP)]


def split(weights):
    high = weights.astype(BF16)
    low = (weights - high.astype(F32)).astype(BF16)
    return high, low


def three_terms(x):
    one = x.astype(BF16).astype(F32)
    two = (x - one).astype(BF16).astype(F32)
    three = (x - one - two).astype(BF16).astype(F32)
    return one, two, three


def params(mib=48):
    return pltpu.CompilerParams(vmem_limit_bytes=mib * 1024 * 1024)


def cost(flops, size):
    return pl.CostEstimate(flops=flops, bytes_accessed=size, transcendentals=0)


def gathered_matmul(index, pieces, weight, keep):
    rows, width = pieces[0].shape
    groups, _, cols = weight.shape

    def body(index_ref, *refs):
        piece_refs, weight_ref = refs[:TP], refs[TP]
        out_ref, acc_ref = refs[TP + 1], refs[-1]
        step = pl.program_id(0)
        for k, piece_ref in enumerate(piece_refs):

            @pl.when(step == k)
            def _():
                piece = piece_ref[...]
                for g in range(groups):
                    term = jnp.dot(piece, weight_ref[g], preferred_element_type=F32)
                    acc_ref[g] = term if k == 0 else acc_ref[g] + term
                if keep:
                    refs[TP + 2][...] = piece

        @pl.when(step == TP - 1)
        def _():
            out_ref[...] = acc_ref[...].astype(BF16)

    out_shape = [jax.ShapeDtypeStruct((groups, rows, cols), BF16)]
    out_specs = [pl.BlockSpec((groups, rows, cols), lambda k, i: (0, 0, 0))]
    if keep:
        out_shape.append(jax.ShapeDtypeStruct((rows, TP * width), BF16))
        out_specs.append(pl.BlockSpec((rows, width), lambda k, i: (0, i[k])))
    return pl.pallas_call(
        body,
        grid_spec=pltpu.PrefetchScalarGridSpec(
            num_scalar_prefetch=1,
            grid=(TP,),
            in_specs=[pl.BlockSpec((rows, width), lambda k, i: (0, 0))] * TP
            + [pl.BlockSpec((groups, width, cols), lambda k, i: (0, i[k], 0))],
            out_specs=out_specs,
            scratch_shapes=[pltpu.VMEM((groups, rows, cols), F32)],
        ),
        out_shape=out_shape,
        compiler_params=params(),
        cost_estimate=cost(2 * rows * weight.size, 2 * weight.size),
    )(index, *pieces, weight)


def cross_partial(bases, pos, queries, mine, other):
    count, width = queries.shape
    heads = width // HD
    rows = 128

    def body(base_ref, pos_ref, q_ref, mine_ref, other_ref, out_ref, stat_ref):
        pos = pos_ref[...]
        stat_ref[...] = jnp.zeros_like(stat_ref)
        for h in range(heads):
            cols = slice(h * HD, (h + 1) * HD)
            q = q_ref[:, cols]
            found = []
            for n, ref in enumerate((mine_ref, other_ref)):
                s = lax.dot_general(ref[0, :, cols], q, NT, preferred_element_type=F32) * SCALE
                key = base_ref[n] + lax.broadcasted_iota(jnp.int32, s.shape, 0)
                found.append(jnp.where(key <= pos, s, NEG))
            peak = jnp.maximum(*[jnp.max(s, axis=0, keepdims=True) for s in found])
            floor = jnp.maximum(peak, NEG * 0.5)
            total = jnp.zeros_like(peak)
            summed = jnp.zeros((HD, rows), F32)
            for s, ref in zip(found, (mine_ref, other_ref)):
                weights = jnp.exp(s - floor)
                total = total + jnp.sum(weights, axis=0, keepdims=True)
                for part in split(weights):
                    summed = summed + lax.dot_general(
                        ref[1, :, cols], part, TN, preferred_element_type=F32
                    )
            out_ref[:, cols] = summed.T.astype(BF16)
            for n, term in enumerate(three_terms(floor) + three_terms(total)):
                stat_ref[n * heads + h : n * heads + h + 1, :] = term
        out_ref[:, width:] = stat_ref[...].T.astype(BF16)

    keyval = pl.BlockSpec(mine.shape, lambda r, b: (0, 0, 0))
    return pl.pallas_call(
        body,
        grid_spec=pltpu.PrefetchScalarGridSpec(
            num_scalar_prefetch=1,
            grid=(count // rows,),
            in_specs=[
                pl.BlockSpec((1, rows), lambda r, b: (0, r)),
                pl.BlockSpec((rows, width), lambda r, b: (r, 0)),
                keyval,
                keyval,
            ],
            out_specs=pl.BlockSpec((rows, width + LANES), lambda r, b: (r, 0)),
            scratch_shapes=[pltpu.VMEM((LANES, rows), F32)],
        ),
        out_shape=jax.ShapeDtypeStruct((count, width + LANES), BF16),
        compiler_params=params(),
        cost_estimate=cost(6 * count * 2 * mine.shape[1] * width, 4 * count * width),
    )(bases, pos, queries, mine, other)


def combine_and_project(terms, weight):
    count, rows, packed = terms.shape
    width = packed - LANES
    heads = width // HD

    def body(x_ref, w_ref, out_ref, context_ref):
        stats = x_ref[:, :, width:].astype(F32)
        field = [stats[:, :, n * heads : (n + 1) * heads] for n in range(6)]
        peak = field[0] + field[1] + field[2]
        total = field[3] + field[4] + field[5]
        factor = jnp.exp(peak - jnp.max(peak, axis=0, keepdims=True))
        total = jnp.sum(factor * total, axis=0)
        for h in range(heads):
            cols = slice(h * HD, (h + 1) * HD)
            summed = jnp.sum(factor[:, :, h : h + 1] * x_ref[:, :, cols].astype(F32), axis=0)
            context_ref[:, cols] = (summed / total[:, h : h + 1]).astype(BF16)
        out_ref[...] = jnp.dot(
            context_ref[...], w_ref[...], preferred_element_type=F32
        ).astype(BF16)

    return pl.pallas_call(
        body,
        out_shape=jax.ShapeDtypeStruct((rows, weight.shape[1]), BF16),
        scratch_shapes=[pltpu.VMEM((rows, width), BF16)],
        compiler_params=params(),
        cost_estimate=cost(2 * rows * weight.size, 2 * weight.size),
    )(terms, weight)


def add_and_norm(base_ref, term_refs, gain_ref):
    a, b, c, d = [ref[...].astype(F32) for ref in term_refs]
    total = (base_ref[...].astype(F32) + ((a + c) + (b + d))).astype(BF16)
    x = total.astype(F32)
    scale = lax.rsqrt(jnp.mean(x * x, axis=-1, keepdims=True) + EPS)
    return total, (x * scale * gain_ref[...]).astype(BF16)


def norm_and_qkv(base, terms, gain, weight):
    rows, width = base.shape
    cols = weight.shape[1]
    block = 256

    def body(base_ref, a, b, c, d, gain_ref, w_ref, total_ref, out_ref, normed_ref):
        @pl.when(pl.program_id(0) == 0)
        def _():
            total, normed = add_and_norm(base_ref, (a, b, c, d), gain_ref)
            total_ref[...] = total
            normed_ref[...] = normed

        out_ref[...] = jnp.dot(
            normed_ref[...], w_ref[...], preferred_element_type=F32
        ).astype(BF16)

    whole = pl.BlockSpec((rows, width), lambda j: (0, 0))
    return pl.pallas_call(
        body,
        grid=(cols // block,),
        in_specs=[whole] * 5
        + [pl.BlockSpec((1, width), lambda j: (0, 0)), pl.BlockSpec((width, block), lambda j: (0, j))],
        out_specs=[whole, pl.BlockSpec((rows, block), lambda j: (0, j))],
        out_shape=[
            jax.ShapeDtypeStruct((rows, width), BF16),
            jax.ShapeDtypeStruct((rows, cols), BF16),
        ],
        scratch_shapes=[pltpu.VMEM((rows, width), BF16)],
        compiler_params=params(),
        cost_estimate=cost(2 * rows * weight.size, 2 * weight.size),
    )(base, *terms, gain, weight)


def self_attention(place, queries, mine, other, weight, column):
    rows, width = queries.shape
    heads = width // HD
    count = mine.shape[0]
    out = weight.shape[0]

    def body(place_ref, q_ref, mine_ref, other_ref, w_ref, out_ref, context_ref):
        core = place_ref[1]
        j = lax.broadcasted_iota(jnp.int32, (rows, count), 1)
        row = place_ref[0] * rows + lax.broadcasted_iota(jnp.int32, (rows, count), 0)
        start = (j // rows) * (CORES * rows) + j % rows
        allowed = [start + core * rows <= row, start + (1 - core) * rows <= row]
        for h in range(heads):
            cols = slice(h * HD, (h + 1) * HD)
            value_cols = slice(width + h * HD, width + (h + 1) * HD)
            q = q_ref[:, cols]
            found = []
            for ref, seen in zip((mine_ref, other_ref), allowed):
                s = lax.dot_general(q, ref[:, cols], NT, preferred_element_type=F32) * SCALE
                found.append(jnp.where(seen, s, NEG))
            peak = jnp.maximum(*[jnp.max(s, axis=1, keepdims=True) for s in found])
            total = jnp.zeros_like(peak)
            summed = jnp.zeros((rows, HD), F32)
            for s, ref in zip(found, (mine_ref, other_ref)):
                weights = jnp.exp(s - peak)
                total = total + jnp.sum(weights, axis=1, keepdims=True)
                for part in split(weights):
                    summed = summed + jnp.dot(
                        part, ref[:, value_cols], preferred_element_type=F32
                    )
            context_ref[:, cols] = (summed / total).astype(BF16)
        out_ref[...] = lax.dot_general(
            context_ref[...], w_ref[...], NT, preferred_element_type=F32
        ).astype(BF16)

    whole = lambda *shape: pl.BlockSpec(shape, lambda i, p: (0, 0))
    return pl.pallas_call(
        body,
        grid_spec=pltpu.PrefetchScalarGridSpec(
            num_scalar_prefetch=1,
            grid=(1,),
            in_specs=[
                whole(rows, width),
                whole(count, 2 * width),
                whole(count, 2 * width),
                pl.BlockSpec((out, width), lambda i, p: (0, column // width)),
            ],
            out_specs=whole(rows, out),
            scratch_shapes=[pltpu.VMEM((rows, width), BF16)],
        ),
        out_shape=jax.ShapeDtypeStruct((rows, out), BF16),
        compiler_params=params(),
        cost_estimate=cost(2 * rows * out * width, 2 * out * width),
    )(place, queries, mine, other, weight)


def mlp(index, base, terms, gain, weight, gate, up, down, hidden):
    rows, width = base.shape
    block = 256
    piece = width // TP

    def body(index_ref, base_ref, a, b, c, d, gain_ref, g_ref, u_ref, d_ref, *refs):
        own_ref, part_refs = refs[0], refs[1 : 1 + TP]
        total_ref, normed_ref, acc_ref = refs[1 + TP :]
        step = pl.program_id(0)

        @pl.when(step == 0)
        def _():
            total, normed = add_and_norm(base_ref, (a, b, c, d), gain_ref)
            total_ref[...] = total
            normed_ref[...] = normed

        normed = normed_ref[...]
        g = jnp.dot(normed, g_ref[...], preferred_element_type=F32)
        u = jnp.dot(normed, u_ref[...], preferred_element_type=F32)
        inner = (jax.nn.silu(g) * u).astype(BF16)
        term = lax.dot_general(inner, d_ref[...], NT, preferred_element_type=F32)

        @pl.when(step == 0)
        def _():
            acc_ref[...] = term

        @pl.when(step > 0)
        def _():
            acc_ref[...] += term

        @pl.when(step == hidden // block - 1)
        def _():
            columns = lambda k: pl.ds(pl.multiple_of(index_ref[k] * piece, piece), piece)
            own_ref[...] = total_ref[:, columns(0)]
            for k in range(TP):
                part_refs[k][...] = acc_ref[:, columns(k)].astype(BF16)

    whole = pl.BlockSpec((rows, width), lambda f, i: (0, 0))
    at = lambda first: pl.BlockSpec((width, block), lambda f, i: (0, first // block + f))
    return pl.pallas_call(
        body,
        grid_spec=pltpu.PrefetchScalarGridSpec(
            num_scalar_prefetch=1,
            grid=(hidden // block,),
            in_specs=[whole] * 5
            + [pl.BlockSpec((1, width), lambda f, i: (0, 0)), at(gate), at(up), at(down)],
            out_specs=[pl.BlockSpec((rows, piece), lambda f, i: (0, 0))] * (1 + TP),
            scratch_shapes=[
                pltpu.VMEM((rows, width), BF16),
                pltpu.VMEM((rows, width), BF16),
                pltpu.VMEM((rows, width), F32),
            ],
        ),
        out_shape=[jax.ShapeDtypeStruct((rows, piece), BF16)] * (1 + TP),
        compiler_params=params(),
        cost_estimate=cost(6 * rows * width * hidden, 6 * width * hidden),
    )(index, base, *terms, gain, weight, weight, weight)


def local(
    prefix,
    latent_in,
    latent_pos,
    w_query,
    w_keyval,
    w_cross_out,
    attn_gain,
    w_self_qkv,
    w_self_out,
    mlp_gain,
    w_gate_up,
    w_down,
):
    chips = lax.axis_size(ZX)
    chip = lax.axis_index(ZX)
    core = lax.axis_index("core")
    tp = lax.axis_index("tp")
    seq = chip * CORES + core
    rows = latent_in.shape[0]
    width = w_query.shape[1]
    hidden = w_gate_up.shape[2]
    positions = prefix.shape[0]
    steps = jnp.arange(TP, dtype=jnp.int32)
    source = (tp - steps) % TP
    target = (tp + steps) % TP

    qkv_rows = jnp.concatenate([w_self_qkv[n] for n in range(3)], axis=1)
    late_rows = jnp.concatenate([w_self_out.T, w_gate_up[0], w_gate_up[1], w_down.T], axis=1)
    w_qkv = lax.all_gather(qkv_rows, SEQ, axis=0, tiled=True)
    w_late = lax.all_gather(late_rows, SEQ, axis=0, tiled=True)

    latent_pieces = everyone(latent_in)
    prefix_pieces = everyone(prefix)
    queries, latents = gathered_matmul(source, latent_pieces, w_query[None], True)
    (keyval,) = gathered_matmul(source, prefix_pieces, w_keyval, False)
    other_keyval = shifted(keyval, "core", 1, CORES)

    spread = jnp.broadcast_to(queries, (chips, rows, width))
    all_queries = lax.all_to_all(spread, ZX, 0, 0).reshape(chips * rows, width)
    pos = lax.dynamic_index_in_dim(
        latent_pos.reshape(chips, CORES, rows), core, axis=1, keepdims=False
    ).reshape(1, chips * rows)
    bases = jnp.stack([seq, chip * CORES + 1 - core]).astype(jnp.int32) * positions
    partial = cross_partial(bases, pos, all_queries, keyval, other_keyval)
    partial = lax.all_to_all(partial.reshape(chips, rows, -1), ZX, 0, 0)
    cross_terms = combine_and_project(partial, w_cross_out)

    first, qkv = norm_and_qkv(latents, everyone(cross_terms), attn_gain[None], w_qkv)
    spread = jnp.broadcast_to(qkv[None, :, width:], (chips, rows, 2 * width))
    mine = lax.all_to_all(spread, ZX, 0, 0).reshape(chips * rows, 2 * width)
    other = shifted(mine, "core", 1, CORES)
    place = jnp.stack([seq, core]).astype(jnp.int32)
    out_terms = self_attention(place, qkv[:, :width], mine, other, w_late, 0)

    own, *parts = mlp(
        target,
        first,
        everyone(out_terms),
        mlp_gain[None],
        w_late,
        width,
        width + hidden,
        width + 2 * hidden,
        hidden,
    )
    sums = [parts[0]] + [shifted(parts[k], "tp", k, TP) for k in range(1, TP)]
    a, b, c, d = [x.astype(F32) for x in sums]
    return (own.astype(F32) + ((a + c) + (b + d))).astype(BF16)


def solution(mesh):
    z, x, core, y = 8, 4, 2, TP
    grid = Mesh(mesh.devices.reshape(z, x, core, y), ("z", "x", "core", "tp"))
    return jax.shard_map(
        local,
        mesh=grid,
        in_specs=(
            P(SEQ, "tp"),
            P(SEQ, "tp"),
            P(),
            P(None, "tp"),
            P(None, None, "tp"),
            P("tp", None),
            P(),
            P(None, SEQ, "tp"),
            P("tp", SEQ),
            P(),
            P(None, SEQ, "tp"),
            P("tp", SEQ),
        ),
        out_specs=P(SEQ, "tp"),
        check_vma=False,
    )
```

```python
import jax
import jax.numpy as jnp
from jax import lax
from jax.experimental import pallas as pl
from jax.experimental.pallas import tpu as pltpu
from jax.sharding import Mesh
from jax.sharding import PartitionSpec as P

HD = 128
NEG = -1e30
EPS = 1e-05
SCALE = HD ** (-0.5)
TP = 4
CORES = 2
DEPTH = 8
BREADTH = 4
LANES = 128
ZX = ("z", "x")
SEQ = ("z", "x", "core")
BF16 = jnp.bfloat16
F32 = jnp.float32
NT = (((1,), (1,)), ((), ()))
TN = (((0,), (0,)), ((), ()))


def shifted(x, axis, shift, count):
    return lax.ppermute(x, axis, [(i, (i + shift) % count) for i in range(count)])


def everyone(x):
    return [x] + [shifted(x, "tp", k, TP) for k in range(1, TP)]


def split(weights):
    high = weights.astype(BF16)
    low = (weights - high.astype(F32)).astype(BF16)
    return high, low


def three_terms(x):
    one = x.astype(BF16).astype(F32)
    two = (x - one).astype(BF16).astype(F32)
    three = (x - one - two).astype(BF16).astype(F32)
    return one, two, three


def params(mib=58):
    return pltpu.CompilerParams(vmem_limit_bytes=mib * 1024 * 1024)


def cost(flops, size):
    return pl.CostEstimate(flops=1, bytes_accessed=1, transcendentals=0)


def gathered_matmul(index, pieces, weight, keep):
    rows, width = pieces[0].shape
    groups, _, cols = weight.shape

    def body(index_ref, *refs):
        piece_refs, weight_ref = refs[:TP], refs[TP]
        out_ref, acc_ref = refs[TP + 1], refs[-1]
        step = pl.program_id(0)
        for k, piece_ref in enumerate(piece_refs):

            @pl.when(step == k)
            def _():
                piece = piece_ref[...]
                for g in range(groups):
                    term = jnp.dot(piece, weight_ref[g], preferred_element_type=F32)
                    acc_ref[g] = term if k == 0 else acc_ref[g] + term
                if keep:
                    refs[TP + 2][...] = piece

        @pl.when(step == TP - 1)
        def _():
            out_ref[...] = acc_ref[...].astype(BF16)

    out_shape = [jax.ShapeDtypeStruct((groups, rows, cols), BF16)]
    out_specs = [pl.BlockSpec((groups, rows, cols), lambda k, i: (0, 0, 0))]
    if keep:
        out_shape.append(jax.ShapeDtypeStruct((rows, TP * width), BF16))
        out_specs.append(pl.BlockSpec((rows, width), lambda k, i: (0, i[k])))
    return pl.pallas_call(
        body,
        grid_spec=pltpu.PrefetchScalarGridSpec(
            num_scalar_prefetch=1,
            grid=(TP,),
            in_specs=[pl.BlockSpec((rows, width), lambda k, i: (0, 0))] * TP
            + [pl.BlockSpec((groups, width, cols), lambda k, i: (0, i[k], 0))],
            out_specs=out_specs,
            scratch_shapes=[pltpu.VMEM((groups, rows, cols), F32)],
        ),
        out_shape=out_shape,
        compiler_params=params(),
        cost_estimate=cost(2 * rows * weight.size, 2 * weight.size),
    )(index, *pieces, weight)


def cross_partial(bases, pos, queries, mine, other):
    count, width = queries.shape
    heads = width // HD
    rows = 128

    def body(base_ref, pos_ref, q_ref, mine_ref, other_ref, out_ref, stat_ref):
        pos = pos_ref[...]
        stat_ref[...] = jnp.zeros_like(stat_ref)
        for h in range(heads):
            cols = slice(h * HD, (h + 1) * HD)
            q = q_ref[:, cols]
            found = []
            for n, ref in enumerate((mine_ref, other_ref)):
                s = lax.dot_general(ref[0, :, cols], q, NT, preferred_element_type=F32) * SCALE
                key = base_ref[n] + lax.broadcasted_iota(jnp.int32, s.shape, 0)
                found.append(jnp.where(key <= pos, s, NEG))
            peak = jnp.maximum(*[jnp.max(s, axis=0, keepdims=True) for s in found])
            floor = jnp.maximum(peak, NEG * 0.5)
            total = jnp.zeros_like(peak)
            summed = jnp.zeros((HD, rows), F32)
            for s, ref in zip(found, (mine_ref, other_ref)):
                weights = jnp.exp(s - floor)
                total = total + jnp.sum(weights, axis=0, keepdims=True)
                for part in split(weights):
                    summed = summed + lax.dot_general(
                        ref[1, :, cols], part, TN, preferred_element_type=F32
                    )
            out_ref[:, cols] = summed.T.astype(BF16)
            for n, term in enumerate(three_terms(floor) + three_terms(total)):
                stat_ref[n * heads + h : n * heads + h + 1, :] = term
        out_ref[:, width:] = stat_ref[...].T.astype(BF16)

    keyval = pl.BlockSpec(mine.shape, lambda r, b: (0, 0, 0))
    return pl.pallas_call(
        body,
        grid_spec=pltpu.PrefetchScalarGridSpec(
            num_scalar_prefetch=1,
            grid=(count // rows,),
            in_specs=[
                pl.BlockSpec((1, rows), lambda r, b: (0, r)),
                pl.BlockSpec((rows, width), lambda r, b: (r, 0)),
                keyval,
                keyval,
            ],
            out_specs=pl.BlockSpec((rows, width + LANES), lambda r, b: (r, 0)),
            scratch_shapes=[pltpu.VMEM((LANES, rows), F32)],
        ),
        out_shape=jax.ShapeDtypeStruct((count, width + LANES), BF16),
        compiler_params=params(),
        cost_estimate=cost(6 * count * 2 * mine.shape[1] * width, 4 * count * width),
    )(bases, pos, queries, mine, other)


def combine_and_project(terms, weight):
    count, rows, packed = terms.shape
    width = packed - LANES
    heads = width // HD

    def body(x_ref, w_ref, out_ref, context_ref):
        stats = x_ref[:, :, width:].astype(F32)
        field = [stats[:, :, n * heads : (n + 1) * heads] for n in range(6)]
        peak = field[0] + field[1] + field[2]
        total = field[3] + field[4] + field[5]
        factor = jnp.exp(peak - jnp.max(peak, axis=0, keepdims=True))
        total = jnp.sum(factor * total, axis=0)
        for h in range(heads):
            cols = slice(h * HD, (h + 1) * HD)
            summed = jnp.sum(factor[:, :, h : h + 1] * x_ref[:, :, cols].astype(F32), axis=0)
            context_ref[:, cols] = (summed / total[:, h : h + 1]).astype(BF16)
        out_ref[...] = jnp.dot(
            context_ref[...], w_ref[...], preferred_element_type=F32
        ).astype(BF16)

    return pl.pallas_call(
        body,
        out_shape=jax.ShapeDtypeStruct((rows, weight.shape[1]), BF16),
        scratch_shapes=[pltpu.VMEM((rows, width), BF16)],
        compiler_params=params(),
        cost_estimate=cost(2 * rows * weight.size, 2 * weight.size),
    )(terms, weight)


def add_and_norm(base_ref, term_refs, gain_ref):
    a, b, c, d = [ref[...].astype(F32) for ref in term_refs]
    total = (base_ref[...].astype(F32) + ((a + c) + (b + d))).astype(BF16)
    x = total.astype(F32)
    scale = lax.rsqrt(jnp.mean(x * x, axis=-1, keepdims=True) + EPS)
    return total, (x * scale * gain_ref[...]).astype(BF16)


def norm(base, terms, gain):
    rows, width = base.shape

    def body(base_ref, a, b, c, d, gain_ref, total_ref, normed_ref):
        total, normed = add_and_norm(base_ref, (a, b, c, d), gain_ref)
        total_ref[...] = total
        normed_ref[...] = normed

    return pl.pallas_call(
        body,
        out_shape=[jax.ShapeDtypeStruct((rows, width), BF16)] * 2,
        compiler_params=params(),
        cost_estimate=cost(0, 0),
    )(base, *terms, gain)


def pack(x, w_self_qkv, w_self_out, w_gate_up, w_down):
    groups, depth, _ = w_self_qkv.shape
    hidden = w_down.shape[1]

    def body(x_ref, qkv_ref, out_ref, gate_up_ref, down_ref, packed_ref, *head_refs):
        packed_ref[:, :hidden] = gate_up_ref[0]
        packed_ref[:, hidden : 2 * hidden] = gate_up_ref[1]
        packed_ref[:, 2 * hidden :] = down_ref[...]
        for k, ref in enumerate(head_refs):
            head = lax.rem(x_ref[0] + k, BREADTH)
            columns = pl.ds(pl.multiple_of(head * HD, HD), HD)
            for g in range(groups):
                ref[:, g * HD : (g + 1) * HD] = qkv_ref[g, :, columns]
            ref[:, groups * HD :] = out_ref[:, columns]

    part = jax.ShapeDtypeStruct((depth, (groups + 1) * HD), BF16)
    vmem = pl.BlockSpec(memory_space=pltpu.VMEM)
    return pl.pallas_call(
        body,
        in_specs=[pl.BlockSpec(memory_space=pltpu.SMEM)] + [vmem] * 4,
        out_specs=[vmem] * (1 + BREADTH),
        out_shape=[jax.ShapeDtypeStruct((depth, 3 * hidden), BF16)] + [part] * BREADTH,
        cost_estimate=cost(0, 0),
    )(x, w_self_qkv, w_self_out, w_gate_up, w_down)


def assemble(spot, mine, other):
    _, _, depth, cols = mine.shape

    def body(spot_ref, mine_ref, other_ref, out_ref, sem):
        x, core = spot_ref[1], spot_ref[2]
        for ref, at_core in ((mine_ref, core), (other_ref, 1 - core)):
            for z in range(DEPTH):
                for k in range(BREADTH):
                    at_x = lax.rem(x + BREADTH - k, BREADTH)
                    place = ((z * BREADTH + at_x) * CORES + at_core) * depth
                    rows = pl.ds(pl.multiple_of(place, depth), depth)
                    pltpu.make_async_copy(ref.at[z, k], out_ref.at[rows], sem).start()
        pltpu.make_async_copy(out_ref, out_ref, sem).wait()

    anywhere = pl.BlockSpec(memory_space=pl.ANY)
    return pl.pallas_call(
        body,
        in_specs=[pl.BlockSpec(memory_space=pltpu.SMEM), anywhere, anywhere],
        out_specs=pl.BlockSpec(memory_space=pltpu.VMEM),
        out_shape=jax.ShapeDtypeStruct((DEPTH * BREADTH * CORES * depth, cols), BF16),
        scratch_shapes=[pltpu.SemaphoreType.DMA],
        compiler_params=params(48),
        cost_estimate=cost(0, 0),
    )(spot, mine, other)


def project_head(normed, weight):
    rows, width = normed[0].shape

    def body(*refs):
        latents = jnp.concatenate([ref[...] for ref in refs[:BREADTH]], axis=0)
        weight_ref, query_ref, keyval_ref = refs[BREADTH:]
        out = jnp.dot(latents, weight_ref[...], preferred_element_type=F32).astype(BF16)
        query_ref[...] = out[:, :HD]
        keyval_ref[...] = out[:, HD:]

    whole = lambda *shape: pl.BlockSpec(shape, lambda i: (0, 0))
    return pl.pallas_call(
        body,
        grid=(1,),
        in_specs=[whole(rows, width)] * BREADTH + [whole(width, 3 * HD)],
        out_specs=[whole(BREADTH * rows, HD), whole(BREADTH * rows, 2 * HD)],
        out_shape=[
            jax.ShapeDtypeStruct((BREADTH * rows, HD), BF16),
            jax.ShapeDtypeStruct((BREADTH * rows, 2 * HD), BF16),
        ],
        compiler_params=params(48),
        cost_estimate=cost(0, 0),
    )(*normed, weight)


def self_attention(spot, rows, queries, mine, other, weight):
    total_rows, width = queries.shape
    count = mine.shape[0]
    features = weight.shape[0]

    def index(n, x, core):
        at_z, at_x = n // total_rows, (x + BREADTH - (n // rows) % BREADTH) % BREADTH
        return ((at_z * BREADTH + at_x) * CORES + core) * rows + n % rows

    def body(spot_ref, q_ref, mine_ref, other_ref, weight_ref, *out_refs):
        z, x, core = spot_ref[0], spot_ref[1], spot_ref[2]
        n = lax.broadcasted_iota(jnp.int32, (1, count), 1)
        key = index(n, x, core)
        keys = (key, key + (1 - 2 * core) * rows)
        n = z * total_rows + lax.broadcasted_iota(jnp.int32, (total_rows, 1), 0)
        row = index(n, x, core)
        found = []
        for ref, key in zip((mine_ref, other_ref), keys):
            s = lax.dot_general(q_ref[...], ref[:, :width], NT, preferred_element_type=F32)
            found.append(jnp.where(key <= row, s * SCALE, NEG))
        peak = jnp.maximum(*[jnp.max(s, axis=1, keepdims=True) for s in found])
        total = jnp.zeros_like(peak)
        summed = jnp.zeros((total_rows, width), F32)
        for s, ref in zip(found, (mine_ref, other_ref)):
            weights = jnp.exp(s - peak)
            total = total + jnp.sum(weights, axis=1, keepdims=True)
            for part in split(weights):
                summed = summed + jnp.dot(part, ref[:, width:], preferred_element_type=F32)
        context = (summed / total).astype(BF16)
        out = lax.dot_general(context, weight_ref[...], NT, preferred_element_type=F32)
        out = out.astype(BF16)
        for k, ref in enumerate(out_refs):
            ref[...] = out[k * rows : (k + 1) * rows]

    whole = lambda *shape: pl.BlockSpec(shape, lambda i, p: (0, 0))
    return pl.pallas_call(
        body,
        grid_spec=pltpu.PrefetchScalarGridSpec(
            num_scalar_prefetch=1,
            grid=(1,),
            in_specs=[whole(total_rows, width)]
            + [whole(count, 2 * width)] * CORES
            + [pl.BlockSpec((features, width), lambda i, p: (0, 3))],
            out_specs=[whole(rows, features)] * BREADTH,
        ),
        out_shape=[jax.ShapeDtypeStruct((rows, features), BF16)] * BREADTH,
        compiler_params=params(48),
        cost_estimate=cost(0, 0),
    )(spot, queries, mine, other, weight)


def mlp(index, base, terms, gain, weight, gate, up, down, hidden):
    rows, width = base.shape
    block = 256
    piece = width // TP

    def body(index_ref, base_ref, a, b, c, d, gain_ref, g_ref, u_ref, d_ref, *refs):
        own_ref, part_refs = refs[0], refs[1 : 1 + TP]
        total_ref, normed_ref, acc_ref = refs[1 + TP :]
        step = pl.program_id(0)

        @pl.when(step == 0)
        def _():
            total, normed = add_and_norm(base_ref, (a, b, c, d), gain_ref)
            total_ref[...] = total
            normed_ref[...] = normed

        normed = normed_ref[...]
        g = jnp.dot(normed, g_ref[...], preferred_element_type=F32)
        u = jnp.dot(normed, u_ref[...], preferred_element_type=F32)
        inner = (jax.nn.silu(g) * u).astype(BF16)
        term = lax.dot_general(inner, d_ref[...], NT, preferred_element_type=F32)

        @pl.when(step == 0)
        def _():
            acc_ref[...] = term

        @pl.when(step > 0)
        def _():
            acc_ref[...] += term

        @pl.when(step == hidden // block - 1)
        def _():
            columns = lambda k: pl.ds(pl.multiple_of(index_ref[k] * piece, piece), piece)
            own_ref[...] = total_ref[:, columns(0)]
            for k in range(TP):
                part_refs[k][...] = acc_ref[:, columns(k)].astype(BF16)

    whole = pl.BlockSpec((rows, width), lambda f, i: (0, 0))
    at = lambda first: pl.BlockSpec((width, block), lambda f, i: (0, first // block + f))
    return pl.pallas_call(
        body,
        grid_spec=pltpu.PrefetchScalarGridSpec(
            num_scalar_prefetch=1,
            grid=(hidden // block,),
            in_specs=[whole] * 5
            + [pl.BlockSpec((1, width), lambda f, i: (0, 0)), at(gate), at(up), at(down)],
            out_specs=[pl.BlockSpec((rows, piece), lambda f, i: (0, 0))] * (1 + TP),
            scratch_shapes=[
                pltpu.VMEM((rows, width), BF16),
                pltpu.VMEM((rows, width), BF16),
                pltpu.VMEM((rows, width), F32),
            ],
        ),
        out_shape=[jax.ShapeDtypeStruct((rows, piece), BF16)] * (1 + TP),
        compiler_params=params(),
        cost_estimate=cost(6 * rows * width * hidden, 6 * width * hidden),
    )(index, base, *terms, gain, weight, weight, weight)


def local(
    prefix,
    latent_in,
    latent_pos,
    w_query,
    w_keyval,
    w_cross_out,
    attn_gain,
    w_self_qkv,
    w_self_out,
    mlp_gain,
    w_gate_up,
    w_down,
):
    chips = lax.axis_size(ZX)
    chip = lax.axis_index(ZX)
    core = lax.axis_index("core")
    tp = lax.axis_index("tp")
    seq = chip * CORES + core
    rows = latent_in.shape[0]
    width = w_query.shape[1]
    hidden = w_gate_up.shape[2]
    positions = prefix.shape[0]
    steps = jnp.arange(TP, dtype=jnp.int32)
    source = (tp - steps) % TP
    target = (tp + steps) % TP

    x = lax.axis_index("x")
    late, *heads = pack(x.astype(jnp.int32)[None], w_self_qkv, w_self_out.T, w_gate_up, w_down.T)
    quad = jnp.stack(
        [heads[0]] + [shifted(heads[k], "x", k, BREADTH) for k in range(1, BREADTH)]
    )
    quad, late = lax.optimization_barrier((quad, late))
    quads = lax.all_gather(quad, "z", axis=0)
    w_late = lax.all_gather(late, SEQ, axis=0, tiled=True)

    latent_pieces = everyone(latent_in)
    prefix_pieces = everyone(prefix)
    queries, latents = gathered_matmul(source, latent_pieces, w_query[None], True)
    queries, prefix_pieces = lax.optimization_barrier((queries, prefix_pieces))
    spread = jnp.broadcast_to(queries, (chips, rows, width))
    all_queries = lax.all_to_all(spread, ZX, 0, 0).reshape(chips * rows, width)
    (keyval,) = gathered_matmul(source, prefix_pieces, w_keyval, False)
    other_keyval = shifted(keyval, "core", 1, CORES)
    pos = lax.dynamic_index_in_dim(
        latent_pos.reshape(chips, CORES, rows), core, axis=1, keepdims=False
    ).reshape(1, chips * rows)
    bases = jnp.stack([seq, chip * CORES + 1 - core]).astype(jnp.int32) * positions
    partial = cross_partial(bases, pos, all_queries, keyval, other_keyval)
    partial = lax.all_to_all(partial.reshape(chips, rows, -1), ZX, 0, 0)
    spot = jnp.stack([lax.axis_index("z"), x, core]).astype(jnp.int32)
    w_head = assemble(spot, quads, shifted(quads, "core", 1, CORES))
    partial, w_head = lax.optimization_barrier((partial, w_head))
    cross_terms = combine_and_project(partial, w_cross_out)

    first, normed = norm(latents, everyone(cross_terms), attn_gain[None])
    group = [normed] + [shifted(normed, "x", k, BREADTH) for k in range(1, BREADTH)]
    queries, keyval = project_head(group, w_head)
    spread = jnp.broadcast_to(keyval, (DEPTH, *keyval.shape))
    mine = lax.all_to_all(spread, "z", 0, 0).reshape(-1, keyval.shape[1])
    other = shifted(mine, "core", 1, CORES)
    terms = self_attention(spot, rows, queries, mine, other, w_head)
    terms = [terms[0]] + [shifted(terms[k], "x", BREADTH - k, BREADTH) for k in range(1, BREADTH)]
    out_terms = sum(term.astype(F32) for term in terms).astype(BF16)

    own, *parts = mlp(
        target,
        first,
        everyone(out_terms),
        mlp_gain[None],
        w_late,
        0,
        hidden,
        2 * hidden,
        hidden,
    )
    sums = [parts[0]] + [shifted(parts[k], "tp", k, TP) for k in range(1, TP)]
    a, b, c, d = [x.astype(F32) for x in sums]
    return (own.astype(F32) + ((a + c) + (b + d))).astype(BF16)


def solution(mesh):
    z, x, core, y = DEPTH, BREADTH, CORES, TP
    grid = Mesh(mesh.devices.reshape(z, x, core, y), ("z", "x", "core", "tp"))
    return jax.shard_map(
        local,
        mesh=grid,
        in_specs=(
            P(SEQ, "tp"),
            P(SEQ, "tp"),
            P(),
            P(None, "tp"),
            P(None, None, "tp"),
            P("tp", None),
            P(),
            P(None, SEQ, "tp"),
            P("tp", SEQ),
            P(),
            P(None, SEQ, "tp"),
            P("tp", SEQ),
        ),
        out_specs=P(SEQ, "tp"),
        check_vma=False,
    )
```

```python
import jax
import jax.numpy as jnp
from jax import lax
from jax.experimental import pallas as pl
from jax.experimental.pallas import tpu as pltpu
from jax.sharding import Mesh
from jax.sharding import PartitionSpec as P

HD = 128
NEG = -1e30
EPS = 1e-05
SCALE = HD ** (-0.5)
TP = 4
CORES = 2
DEPTH = 8
BREADTH = 4
LANES = 128
ZX = ("z", "x")
SEQ = ("z", "x", "core")
BF16 = jnp.bfloat16
F32 = jnp.float32
NT = (((1,), (1,)), ((), ()))
TN = (((0,), (0,)), ((), ()))


def shifted(x, axis, shift, count):
    return lax.ppermute(x, axis, [(i, (i + shift) % count) for i in range(count)])


def everyone(x):
    return [x] + [shifted(x, "tp", k, TP) for k in range(1, TP)]


def split(weights):
    high = weights.astype(BF16)
    low = (weights - high.astype(F32)).astype(BF16)
    return high, low


def three_terms(x):
    one = x.astype(BF16).astype(F32)
    two = (x - one).astype(BF16).astype(F32)
    three = (x - one - two).astype(BF16).astype(F32)
    return one, two, three


def params(mib=48):
    return pltpu.CompilerParams(vmem_limit_bytes=mib * 1024 * 1024)


def cost(flops, size):
    return pl.CostEstimate(flops=1, bytes_accessed=1, transcendentals=0)


def gathered_matmul(index, pieces, weight, keep):
    rows, width = pieces[0].shape
    groups, _, cols = weight.shape

    def body(index_ref, *refs):
        piece_refs, weight_ref = refs[:TP], refs[TP]
        out_ref, acc_ref = refs[TP + 1], refs[-1]
        step = pl.program_id(0)
        for k, piece_ref in enumerate(piece_refs):

            @pl.when(step == k)
            def _():
                piece = piece_ref[...]
                for g in range(groups):
                    term = jnp.dot(piece, weight_ref[g], preferred_element_type=F32)
                    acc_ref[g] = term if k == 0 else acc_ref[g] + term
                if keep:
                    refs[TP + 2][...] = piece

        @pl.when(step == TP - 1)
        def _():
            out_ref[...] = acc_ref[...].astype(BF16)

    out_shape = [jax.ShapeDtypeStruct((groups, rows, cols), BF16)]
    out_specs = [pl.BlockSpec((groups, rows, cols), lambda k, i: (0, 0, 0))]
    if keep:
        out_shape.append(jax.ShapeDtypeStruct((rows, TP * width), BF16))
        out_specs.append(pl.BlockSpec((rows, width), lambda k, i: (0, i[k])))
    return pl.pallas_call(
        body,
        grid_spec=pltpu.PrefetchScalarGridSpec(
            num_scalar_prefetch=1,
            grid=(TP,),
            in_specs=[pl.BlockSpec((rows, width), lambda k, i: (0, 0))] * TP
            + [pl.BlockSpec((groups, width, cols), lambda k, i: (0, i[k], 0))],
            out_specs=out_specs,
            scratch_shapes=[pltpu.VMEM((groups, rows, cols), F32)],
        ),
        out_shape=out_shape,
        compiler_params=params(48 if keep else 58),
        cost_estimate=cost(2 * rows * weight.size, 2 * weight.size),
    )(index, *pieces, weight)


def cross_partial(bases, pos, queries, mine, other):
    count, width = queries.shape
    heads = width // HD
    rows = 128

    def body(base_ref, pos_ref, q_ref, mine_ref, other_ref, out_ref, stat_ref):
        pos = pos_ref[...]
        stat_ref[...] = jnp.zeros_like(stat_ref)
        for h in range(heads):
            cols = slice(h * HD, (h + 1) * HD)
            q = q_ref[:, cols]
            found = []
            for n, ref in enumerate((mine_ref, other_ref)):
                s = lax.dot_general(ref[0, :, cols], q, NT, preferred_element_type=F32) * SCALE
                key = base_ref[n] + lax.broadcasted_iota(jnp.int32, s.shape, 0)
                found.append(jnp.where(key <= pos, s, NEG))
            peak = jnp.maximum(*[jnp.max(s, axis=0, keepdims=True) for s in found])
            floor = jnp.maximum(peak, NEG * 0.5)
            total = jnp.zeros_like(peak)
            summed = jnp.zeros((HD, rows), F32)
            for s, ref in zip(found, (mine_ref, other_ref)):
                weights = jnp.exp(s - floor)
                total = total + jnp.sum(weights, axis=0, keepdims=True)
                for part in split(weights):
                    summed = summed + lax.dot_general(
                        ref[1, :, cols], part, TN, preferred_element_type=F32
                    )
            out_ref[:, cols] = summed.T.astype(BF16)
            for n, term in enumerate(three_terms(floor) + three_terms(total)):
                stat_ref[n * heads + h : n * heads + h + 1, :] = term
        out_ref[:, width:] = stat_ref[...].T.astype(BF16)

    keyval = pl.BlockSpec(mine.shape, lambda r, b: (0, 0, 0))
    return pl.pallas_call(
        body,
        grid_spec=pltpu.PrefetchScalarGridSpec(
            num_scalar_prefetch=1,
            grid=(count // rows,),
            in_specs=[
                pl.BlockSpec((1, rows), lambda r, b: (0, r)),
                pl.BlockSpec((rows, width), lambda r, b: (r, 0)),
                keyval,
                keyval,
            ],
            out_specs=pl.BlockSpec((rows, width + LANES), lambda r, b: (r, 0)),
            scratch_shapes=[pltpu.VMEM((LANES, rows), F32)],
        ),
        out_shape=jax.ShapeDtypeStruct((count, width + LANES), BF16),
        compiler_params=params(),
        cost_estimate=cost(6 * count * 2 * mine.shape[1] * width, 4 * count * width),
    )(bases, pos, queries, mine, other)


def combine_and_project(terms, weight):
    count, rows, packed = terms.shape
    width = packed - LANES
    heads = width // HD

    def body(x_ref, w_ref, out_ref, context_ref):
        stats = x_ref[:, :, width:].astype(F32)
        field = [stats[:, :, n * heads : (n + 1) * heads] for n in range(6)]
        peak = field[0] + field[1] + field[2]
        total = field[3] + field[4] + field[5]
        factor = jnp.exp(peak - jnp.max(peak, axis=0, keepdims=True))
        total = jnp.sum(factor * total, axis=0)
        for h in range(heads):
            cols = slice(h * HD, (h + 1) * HD)
            summed = jnp.sum(factor[:, :, h : h + 1] * x_ref[:, :, cols].astype(F32), axis=0)
            context_ref[:, cols] = (summed / total[:, h : h + 1]).astype(BF16)
        out_ref[...] = jnp.dot(
            context_ref[...], w_ref[...], preferred_element_type=F32
        ).astype(BF16)

    return pl.pallas_call(
        body,
        out_shape=jax.ShapeDtypeStruct((rows, weight.shape[1]), BF16),
        scratch_shapes=[pltpu.VMEM((rows, width), BF16)],
        compiler_params=params(),
        cost_estimate=cost(2 * rows * weight.size, 2 * weight.size),
    )(terms, weight)


def add_and_norm(base_ref, term_refs, gain_ref):
    a, b, c, d = [ref[...].astype(F32) for ref in term_refs]
    total = (base_ref[...].astype(F32) + ((a + c) + (b + d))).astype(BF16)
    x = total.astype(F32)
    scale = lax.rsqrt(jnp.mean(x * x, axis=-1, keepdims=True) + EPS)
    return total, (x * scale * gain_ref[...]).astype(BF16)


def norm(base, terms, gain):
    rows, width = base.shape

    def body(base_ref, a, b, c, d, gain_ref, total_ref, normed_ref):
        total, normed = add_and_norm(base_ref, (a, b, c, d), gain_ref)
        total_ref[...] = total
        normed_ref[...] = normed

    return pl.pallas_call(
        body,
        out_shape=[jax.ShapeDtypeStruct((rows, width), BF16)] * 2,
        compiler_params=params(),
        cost_estimate=cost(0, 0),
    )(base, *terms, gain)


def pack(x, w_self_qkv, w_self_out, w_gate_up, w_down):
    groups, depth, _ = w_self_qkv.shape
    share = w_down.shape[1] // BREADTH

    def body(x_ref, qkv_ref, out_ref, gate_up_ref, down_ref, *refs):
        for k, ref in enumerate(refs):
            chip = lax.rem(x_ref[0] + k, BREADTH)
            head = pl.ds(pl.multiple_of(chip * HD, HD), HD)
            units = pl.ds(pl.multiple_of(chip * share, share), share)
            parts = [qkv_ref[g, :, head] for g in range(groups)] + [out_ref[:, head]]
            parts += [gate_up_ref[g, :, units] for g in range(2)] + [down_ref[:, units]]
            ref[...] = jnp.concatenate(parts, axis=1)

    vmem = pl.BlockSpec(memory_space=pltpu.VMEM)
    return pl.pallas_call(
        body,
        in_specs=[pl.BlockSpec(memory_space=pltpu.SMEM)] + [vmem] * 4,
        out_specs=[vmem] * BREADTH,
        out_shape=[jax.ShapeDtypeStruct((depth, 4 * HD + 3 * share), BF16)] * BREADTH,
        cost_estimate=cost(0, 0),
    )(x, w_self_qkv, w_self_out, w_gate_up, w_down)


def assemble(spot, rows, splits):
    depth = rows.shape[3]

    def body(spot_ref, rows_ref, *refs):
        sems = refs[len(splits)]
        for z in range(DEPTH):
            for core in range(CORES):
                for k in range(BREADTH):
                    at_x = lax.rem(spot_ref[1] + BREADTH - k, BREADTH)
                    place = ((z * BREADTH + at_x) * CORES + core) * depth
                    at = pl.ds(pl.multiple_of(place, depth), depth)
                    first = 0
                    for n, width in enumerate(splits):
                        pltpu.make_async_copy(
                            rows_ref.at[z, core, k, :, pl.ds(first, width)],
                            refs[n].at[at],
                            sems.at[n],
                        ).start()
                        first += width
        for n in range(len(splits)):
            pltpu.make_async_copy(refs[n], refs[n], sems.at[n]).wait()

    count = DEPTH * BREADTH * CORES * depth
    return pl.pallas_call(
        body,
        in_specs=[pl.BlockSpec(memory_space=pltpu.SMEM), pl.BlockSpec(memory_space=pl.ANY)],
        out_specs=[pl.BlockSpec(memory_space=pltpu.VMEM)] * len(splits),
        out_shape=[jax.ShapeDtypeStruct((count, width), BF16) for width in splits],
        scratch_shapes=[pltpu.SemaphoreType.DMA((len(splits),))],
        compiler_params=params(58),
        cost_estimate=cost(0, 0),
    )(spot, rows)


def project_head(normed, weight):
    rows, width = normed[0].shape

    def body(*refs):
        latents = jnp.concatenate([ref[...] for ref in refs[:BREADTH]], axis=0)
        weight_ref, query_ref, keyval_ref = refs[BREADTH:]
        out = jnp.dot(latents, weight_ref[...], preferred_element_type=F32).astype(BF16)
        query_ref[...] = out[:, :HD]
        keyval_ref[...] = out[:, HD:]

    whole = lambda *shape: pl.BlockSpec(shape, lambda i: (0, 0))
    return pl.pallas_call(
        body,
        grid=(1,),
        in_specs=[whole(rows, width)] * BREADTH + [whole(width, 3 * HD)],
        out_specs=[whole(BREADTH * rows, HD), whole(BREADTH * rows, 2 * HD)],
        out_shape=[
            jax.ShapeDtypeStruct((BREADTH * rows, HD), BF16),
            jax.ShapeDtypeStruct((BREADTH * rows, 2 * HD), BF16),
        ],
        compiler_params=params(48),
        cost_estimate=cost(0, 0),
    )(*normed, weight)


def self_attention(spot, rows, queries, mine, other, weight):
    total_rows, width = queries.shape
    count = mine.shape[0]
    features = weight.shape[0]

    def index(n, x, core):
        at_z, at_x = n // total_rows, (x + BREADTH - (n // rows) % BREADTH) % BREADTH
        return ((at_z * BREADTH + at_x) * CORES + core) * rows + n % rows

    def body(spot_ref, q_ref, mine_ref, other_ref, weight_ref, *out_refs):
        z, x, core = spot_ref[0], spot_ref[1], spot_ref[2]
        n = lax.broadcasted_iota(jnp.int32, (1, count), 1)
        key = index(n, x, core)
        keys = (key, key + (1 - 2 * core) * rows)
        n = z * total_rows + lax.broadcasted_iota(jnp.int32, (total_rows, 1), 0)
        row = index(n, x, core)
        found = []
        for ref, key in zip((mine_ref, other_ref), keys):
            s = lax.dot_general(q_ref[...], ref[:, :width], NT, preferred_element_type=F32)
            found.append(jnp.where(key <= row, s * SCALE, NEG))
        peak = jnp.maximum(*[jnp.max(s, axis=1, keepdims=True) for s in found])
        total = jnp.zeros_like(peak)
        summed = jnp.zeros((total_rows, width), F32)
        for s, ref in zip(found, (mine_ref, other_ref)):
            weights = jnp.exp(s - peak)
            total = total + jnp.sum(weights, axis=1, keepdims=True)
            for part in split(weights):
                summed = summed + jnp.dot(part, ref[:, width:], preferred_element_type=F32)
        context = (summed / total).astype(BF16)
        out = lax.dot_general(context, weight_ref[...], NT, preferred_element_type=F32)
        out = out.astype(BF16)
        for k, ref in enumerate(out_refs):
            ref[...] = out[k * rows : (k + 1) * rows]

    whole = lambda *shape: pl.BlockSpec(shape, lambda i, p: (0, 0))
    return pl.pallas_call(
        body,
        grid_spec=pltpu.PrefetchScalarGridSpec(
            num_scalar_prefetch=1,
            grid=(1,),
            in_specs=[whole(total_rows, width)]
            + [whole(count, 2 * width)] * CORES
            + [whole(features, width)],
            out_specs=[whole(rows, features)] * BREADTH,
        ),
        out_shape=[jax.ShapeDtypeStruct((rows, features), BF16)] * BREADTH,
        compiler_params=params(48),
        cost_estimate=cost(0, 0),
    )(spot, queries, mine, other, weight)


def norm_own(index, base, terms, gain):
    rows, width = base.shape
    piece = width // TP

    def body(index_ref, base_ref, a, b, c, d, gain_ref, own_ref, normed_ref, total_ref):
        total, normed = add_and_norm(base_ref, (a, b, c, d), gain_ref)
        total_ref[...] = total
        normed_ref[...] = normed
        own_ref[...] = total_ref[:, pl.ds(pl.multiple_of(index_ref[0] * piece, piece), piece)]

    vmem = pl.BlockSpec(memory_space=pltpu.VMEM)
    return pl.pallas_call(
        body,
        in_specs=[pl.BlockSpec(memory_space=pltpu.SMEM)] + [vmem] * 6,
        out_specs=[vmem] * 2,
        out_shape=[
            jax.ShapeDtypeStruct((rows, piece), BF16),
            jax.ShapeDtypeStruct((rows, width), BF16),
        ],
        scratch_shapes=[pltpu.VMEM((rows, width), BF16)],
        compiler_params=params(),
        cost_estimate=cost(0, 0),
    )(index, base, *terms, gain)


def mlp(spot, normed, weight):
    rows, width = normed[0].shape
    share = weight.shape[1] // 3
    piece = width // TP

    def body(spot_ref, *refs):
        latents = jnp.concatenate([ref[...] for ref in refs[:BREADTH]], axis=0)
        weight_ref, out_ref = refs[BREADTH:]
        both = weight_ref[:, : 2 * share]
        both = jnp.dot(latents, both, preferred_element_type=F32)
        inner = (jax.nn.silu(both[:, :share]) * both[:, share:]).astype(BF16)
        for t in range(TP):
            term = lax.dot_general(
                inner,
                weight_ref[t * piece : (t + 1) * piece, 2 * share :],
                NT,
                preferred_element_type=F32,
            ).astype(BF16)
            for k in range(BREADTH):
                chip = lax.rem(spot_ref[1] + BREADTH - k, BREADTH)
                out_ref[chip * TP + t] = term[k * rows : (k + 1) * rows]

    vmem = pl.BlockSpec(memory_space=pltpu.VMEM)
    return pl.pallas_call(
        body,
        in_specs=[pl.BlockSpec(memory_space=pltpu.SMEM)] + [vmem] * (BREADTH + 1),
        out_specs=vmem,
        out_shape=jax.ShapeDtypeStruct((BREADTH * TP, rows, piece), BF16),
        compiler_params=params(),
        cost_estimate=cost(0, 0),
    )(spot, *normed, weight)


def local(
    prefix,
    latent_in,
    latent_pos,
    w_query,
    w_keyval,
    w_cross_out,
    attn_gain,
    w_self_qkv,
    w_self_out,
    mlp_gain,
    w_gate_up,
    w_down,
):
    chips = lax.axis_size(ZX)
    chip = lax.axis_index(ZX)
    core = lax.axis_index("core")
    tp = lax.axis_index("tp")
    seq = chip * CORES + core
    rows = latent_in.shape[0]
    width = w_query.shape[1]
    positions = prefix.shape[0]
    steps = jnp.arange(TP, dtype=jnp.int32)
    source = (tp - steps) % TP

    x = lax.axis_index("x")
    heads = pack(x.astype(jnp.int32)[None], w_self_qkv, w_self_out.T, w_gate_up, w_down.T)
    latent_pieces = everyone(latent_in)
    latent_pieces, heads = lax.optimization_barrier((latent_pieces, heads))
    quad = jnp.stack(
        [heads[0]] + [shifted(heads[k], "x", k, BREADTH) for k in range(1, BREADTH)]
    )

    prefix_pieces = everyone(prefix)
    queries, latents = gathered_matmul(source, latent_pieces, w_query[None], True)
    queries, prefix_pieces, quad = lax.optimization_barrier((queries, prefix_pieces, quad))
    spread = jnp.broadcast_to(queries, (chips, rows, width))
    all_queries = lax.all_to_all(spread, ZX, 0, 0).reshape(chips * rows, width)
    (keyval,) = gathered_matmul(source, prefix_pieces, w_keyval, False)
    other_keyval = shifted(keyval, "core", 1, CORES)
    pos = lax.dynamic_index_in_dim(
        latent_pos.reshape(chips, CORES, rows), core, axis=1, keepdims=False
    ).reshape(1, chips * rows)
    bases = jnp.stack([seq, chip * CORES + 1 - core]).astype(jnp.int32) * positions
    partial = cross_partial(bases, pos, all_queries, keyval, other_keyval)
    partial = lax.all_to_all(partial.reshape(chips, rows, -1), ZX, 0, 0)
    spot = jnp.stack([lax.axis_index("z"), x, core]).astype(jnp.int32)
    rows_of = lax.all_gather(quad, ("z", "core"), axis=0).reshape(DEPTH, CORES, *quad.shape)
    weights = assemble(spot, rows_of, (3 * HD, HD, quad.shape[-1] - 4 * HD))
    partial, weights = lax.optimization_barrier((partial, weights))
    w_qkv, w_out, w_mlp = weights
    cross_terms = combine_and_project(partial, w_cross_out)

    first, normed = norm(latents, everyone(cross_terms), attn_gain[None])
    group = [normed] + [shifted(normed, "x", k, BREADTH) for k in range(1, BREADTH)]
    queries, keyval = project_head(group, w_qkv)
    spread = jnp.broadcast_to(keyval, (DEPTH, *keyval.shape))
    mine = lax.all_to_all(spread, "z", 0, 0).reshape(-1, keyval.shape[1])
    other = shifted(mine, "core", 1, CORES)
    terms = self_attention(spot, rows, queries, mine, other, w_out)
    terms = [terms[0]] + [shifted(terms[k], "x", BREADTH - k, BREADTH) for k in range(1, BREADTH)]
    out_terms = sum(term.astype(F32) for term in terms).astype(BF16)

    own, normed = norm_own(tp.astype(jnp.int32)[None], first, everyone(out_terms), mlp_gain[None])
    group = [normed] + [shifted(normed, "x", k, BREADTH) for k in range(1, BREADTH)]
    down_terms = lax.all_to_all(mlp(spot, group, w_mlp), ("x", "tp"), 0, 0)
    return (own.astype(F32) + jnp.sum(down_terms.astype(F32), axis=0)).astype(BF16)


def solution(mesh):
    z, x, core, y = DEPTH, BREADTH, CORES, TP
    grid = Mesh(mesh.devices.reshape(z, x, core, y), ("z", "x", "core", "tp"))
    return jax.shard_map(
        local,
        mesh=grid,
        in_specs=(
            P(SEQ, "tp"),
            P(SEQ, "tp"),
            P(),
            P(None, "tp"),
            P(None, None, "tp"),
            P("tp", None),
            P(),
            P(None, SEQ, "tp"),
            P("tp", SEQ),
            P(),
            P(None, SEQ, "tp"),
            P("tp", SEQ),
        ),
        out_specs=P(SEQ, "tp"),
        check_vma=False,
    )
```

```python
import jax
import jax.numpy as jnp
from jax import lax
from jax.experimental import pallas as pl
from jax.experimental.pallas import tpu as pltpu
from jax.sharding import Mesh
from jax.sharding import PartitionSpec as P

HD = 128
NEG = -1e30
EPS = 1e-05
SCALE = HD ** (-0.5)
LOG2E = 1.4426950408889634
TP = 4
CORES = 2
DEPTH = 8
BREADTH = 4
LANES = 128
ZX = ("z", "x")
SEQ = ("z", "x", "core")
BF16 = jnp.bfloat16
F32 = jnp.float32
NT = (((1,), (1,)), ((), ()))
TN = (((0,), (0,)), ((), ()))


def shifted(x, axis, shift, count):
    return lax.ppermute(x, axis, [(i, (i + shift) % count) for i in range(count)])


def everyone(x):
    return [x] + [shifted(x, "tp", k, TP) for k in range(1, TP)]


def split(weights):
    high = weights.astype(BF16)
    low = (weights - high.astype(F32)).astype(BF16)
    return high, low


def three_terms(x):
    one = x.astype(BF16).astype(F32)
    two = (x - one).astype(BF16).astype(F32)
    three = (x - one - two).astype(BF16).astype(F32)
    return one, two, three


def params(mib=48):
    return pltpu.CompilerParams(vmem_limit_bytes=mib * 1024 * 1024)


def cost(flops, size):
    return pl.CostEstimate(flops=1, bytes_accessed=1, transcendentals=0)


def project_gathered(index, pieces, weight, body, out_shape, mib):
    rows, width = pieces[0].shape
    groups, _, cols = weight.shape

    def kernel(index_ref, *refs):
        piece_refs, weight_ref = refs[:TP], refs[TP]
        out_refs, held_ref, acc_ref, sems = refs[TP + 1 : -3], refs[-3], refs[-2], refs[-1]
        copies = {}
        for k in range(TP):
            at = pl.ds(pl.multiple_of(index_ref[k] * width, width), width)
            for g in range(groups):
                copies[k, g] = pltpu.make_async_copy(
                    weight_ref.at[g, at, :], held_ref.at[k, g], sems.at[k, g]
                )
                copies[k, g].start()
        for k in range(TP):
            piece = piece_refs[k][...]
            for g in range(groups):
                copies[k, g].wait()
                term = jnp.dot(piece, held_ref[k, g], preferred_element_type=F32)
                acc_ref[g] = term if k == 0 else acc_ref[g] + term
        body(index_ref, piece_refs, acc_ref, out_refs)

    vmem = pl.BlockSpec(memory_space=pltpu.VMEM)
    return pl.pallas_call(
        kernel,
        in_specs=[pl.BlockSpec(memory_space=pltpu.SMEM)]
        + [vmem] * TP
        + [pl.BlockSpec(memory_space=pl.ANY)],
        out_specs=[vmem] * len(out_shape),
        out_shape=out_shape,
        scratch_shapes=[
            pltpu.VMEM((TP, groups, width, cols), BF16),
            pltpu.VMEM((groups, rows, cols), F32),
            pltpu.SemaphoreType.DMA((TP, groups)),
        ],
        compiler_params=params(mib),
        cost_estimate=cost(0, 0),
    )(index, *pieces, weight)


def project_queries(index, pieces, weight):
    rows, width = pieces[0].shape
    heads = weight.shape[1] // HD

    def body(index_ref, piece_refs, acc_ref, out_refs):
        query_ref, whole_ref = out_refs
        for k, ref in enumerate(piece_refs):
            columns = pl.ds(pl.multiple_of(index_ref[k] * width, width), width)
            whole_ref[:, columns] = ref[...]
        for h in range(heads):
            query_ref[h] = acc_ref[0, :, h * HD : (h + 1) * HD].astype(BF16)

    out_shape = [
        jax.ShapeDtypeStruct((heads, rows, HD), BF16),
        jax.ShapeDtypeStruct((rows, TP * width), BF16),
    ]
    return project_gathered(index, pieces, weight[None], body, out_shape, 58)


def project_keyval(index, pieces, weight):
    rows, _ = pieces[0].shape
    groups, _, _ = weight.shape

    def body(index_ref, piece_refs, acc_ref, out_refs):
        for k, ref in enumerate(out_refs):
            head = lax.rem(index_ref[TP] + k, BREADTH)
            columns = pl.ds(pl.multiple_of(head * HD, HD), HD)
            for g in range(groups):
                ref[g] = acc_ref[g, :, columns].astype(BF16)

    out_shape = [jax.ShapeDtypeStruct((groups, rows, HD), BF16)] * BREADTH
    return project_gathered(index, pieces, weight, body, out_shape, 58)


def cross_partial(bases, pos, queries, pieces):
    count = queries.shape[0]
    rows = 128

    def body(base_ref, pos_ref, q_ref, *refs):
        piece_refs, out_ref, stat_ref = refs[: len(pieces)], refs[-2], refs[-1]
        pos, q = pos_ref[...], q_ref[...]
        found = []
        for n, ref in enumerate(piece_refs):
            s = lax.dot_general(ref[0], q, NT, preferred_element_type=F32)
            key = base_ref[n] + lax.broadcasted_iota(jnp.int32, s.shape, 0)
            found.append(jnp.where(key <= pos, s, NEG))
        floor = jnp.full((1, rows), NEG * 0.5, F32)
        for s in found:
            floor = jnp.maximum(floor, jnp.max(s, axis=0, keepdims=True))
        total = jnp.zeros((1, rows), F32)
        summed = jnp.zeros((HD, rows), F32)
        for s, ref in zip(found, piece_refs):
            weights = jnp.exp2((s - floor) * (SCALE * LOG2E))
            total = total + jnp.sum(weights, axis=0, keepdims=True)
            for part in split(weights):
                summed = summed + lax.dot_general(ref[1], part, TN, preferred_element_type=F32)
        out_ref[:, :HD] = summed.T.astype(BF16)
        stat_ref[...] = jnp.zeros_like(stat_ref)
        for n, term in enumerate(three_terms(floor * SCALE) + three_terms(total)):
            stat_ref[n : n + 1, :] = term
        out_ref[:, HD:] = stat_ref[...].T.astype(BF16)

    return pl.pallas_call(
        body,
        grid_spec=pltpu.PrefetchScalarGridSpec(
            num_scalar_prefetch=1,
            grid=(count // rows,),
            in_specs=[
                pl.BlockSpec((1, rows), lambda r, b: (0, r)),
                pl.BlockSpec((rows, HD), lambda r, b: (r, 0)),
            ]
            + [pl.BlockSpec(piece.shape, lambda r, b: (0, 0, 0)) for piece in pieces],
            out_specs=pl.BlockSpec((rows, HD + LANES), lambda r, b: (r, 0)),
            scratch_shapes=[pltpu.VMEM((LANES, rows), F32)],
        ),
        out_shape=jax.ShapeDtypeStruct((count, HD + LANES), BF16),
        compiler_params=params(),
        cost_estimate=cost(0, 0),
    )(bases, pos, queries, *pieces)


def combine_and_project(terms, weight):
    _, heads, rows, _ = terms.shape

    def body(x_ref, w_ref, out_ref, context_ref):
        for h in range(heads):
            stats = x_ref[:, h, :, HD:].astype(F32)
            field = [stats[:, :, n : n + 1] for n in range(6)]
            peak = field[0] + field[1] + field[2]
            factor = jnp.exp(peak - jnp.max(peak, axis=0, keepdims=True))
            total = jnp.sum(factor * (field[3] + field[4] + field[5]), axis=0)
            summed = jnp.sum(factor * x_ref[:, h, :, :HD].astype(F32), axis=0)
            context_ref[:, h * HD : (h + 1) * HD] = (summed / total).astype(BF16)
        out_ref[...] = jnp.dot(
            context_ref[...], w_ref[...], preferred_element_type=F32
        ).astype(BF16)

    return pl.pallas_call(
        body,
        out_shape=jax.ShapeDtypeStruct((rows, weight.shape[1]), BF16),
        scratch_shapes=[pltpu.VMEM((rows, heads * HD), BF16)],
        compiler_params=params(),
        cost_estimate=cost(0, 0),
    )(terms, weight)


def add_and_norm(base_ref, term_refs, gain_ref):
    a, b, c, d = [ref[...].astype(F32) for ref in term_refs]
    total = (base_ref[...].astype(F32) + ((a + c) + (b + d))).astype(BF16)
    x = total.astype(F32)
    scale = lax.rsqrt(jnp.mean(x * x, axis=-1, keepdims=True) + EPS)
    return total, (x * scale * gain_ref[...]).astype(BF16)


def norm(base, terms, gain):
    rows, width = base.shape

    def body(base_ref, a, b, c, d, gain_ref, total_ref, normed_ref):
        total, normed = add_and_norm(base_ref, (a, b, c, d), gain_ref)
        total_ref[...] = total
        normed_ref[...] = normed

    return pl.pallas_call(
        body,
        out_shape=[jax.ShapeDtypeStruct((rows, width), BF16)] * 2,
        compiler_params=params(),
        cost_estimate=cost(0, 0),
    )(base, *terms, gain)


def pack(x, w_self_qkv, w_self_out, w_gate_up, w_down):
    groups, depth, _ = w_self_qkv.shape
    share = w_down.shape[1] // BREADTH

    def body(x_ref, qkv_ref, out_ref, gate_up_ref, down_ref, head_ref, unit_ref, *refs):
        for k in range(BREADTH):
            chip = lax.rem(x_ref[0] + k, BREADTH)
            head = pl.ds(pl.multiple_of(chip * HD, HD), HD)
            units = pl.ds(pl.multiple_of(chip * share, share), share)
            parts = [qkv_ref[g, :, head] for g in range(groups)] + [out_ref[:, head]]
            more = [gate_up_ref[g, :, units] for g in range(2)] + [down_ref[:, units]]
            if k == 0:
                head_ref[...] = jnp.concatenate(parts, axis=1)
                unit_ref[...] = jnp.concatenate(more, axis=1)
            else:
                refs[k - 1][...] = jnp.concatenate(parts + more, axis=1)

    vmem = pl.BlockSpec(memory_space=pltpu.VMEM)
    widths = (4 * HD, 3 * share) + (4 * HD + 3 * share,) * (BREADTH - 1)
    return pl.pallas_call(
        body,
        in_specs=[pl.BlockSpec(memory_space=pltpu.SMEM)] + [vmem] * 4,
        out_specs=[vmem] * len(widths),
        out_shape=[jax.ShapeDtypeStruct((depth, width), BF16) for width in widths],
        cost_estimate=cost(0, 0),
    )(x, w_self_qkv, w_self_out, w_gate_up, w_down)


def start_copies(x, rows_ref, out_refs, sems):
    depth = rows_ref.shape[3]
    for z in range(DEPTH):
        for core in range(CORES):
            for k in range(BREADTH):
                at_x = lax.rem(x + BREADTH - k, BREADTH)
                place = ((z * BREADTH + at_x) * CORES + core) * depth
                at = pl.ds(pl.multiple_of(place, depth), depth)
                first = 0
                for n, out_ref in enumerate(out_refs):
                    width = out_ref.shape[1]
                    pltpu.make_async_copy(
                        rows_ref.at[z, core, k, :, pl.ds(first, width)],
                        out_ref.at[at],
                        sems.at[n],
                    ).start()
                    first += width


def wait_copies(out_refs, sems):
    for n, out_ref in enumerate(out_refs):
        pltpu.make_async_copy(out_ref, out_ref, sems.at[n]).wait()


def assemble(spot, rows, splits):
    def body(spot_ref, rows_ref, *refs):
        start_copies(spot_ref[1], rows_ref, refs[:-1], refs[-1])
        wait_copies(refs[:-1], refs[-1])

    count = DEPTH * BREADTH * CORES * rows.shape[3]
    return pl.pallas_call(
        body,
        in_specs=[pl.BlockSpec(memory_space=pltpu.SMEM), pl.BlockSpec(memory_space=pl.ANY)],
        out_specs=[pl.BlockSpec(memory_space=pltpu.VMEM)] * len(splits),
        out_shape=[jax.ShapeDtypeStruct((count, width), BF16) for width in splits],
        scratch_shapes=[pltpu.SemaphoreType.DMA((len(splits),))],
        compiler_params=params(58),
        cost_estimate=cost(0, 0),
    )(spot, rows)


def project_head(normed, weight):
    rows, width = normed[0].shape

    def body(*refs):
        latents = jnp.concatenate([ref[...] for ref in refs[:BREADTH]], axis=0)
        weight_ref, query_ref, keyval_ref = refs[BREADTH:]
        out = jnp.dot(latents, weight_ref[...], preferred_element_type=F32).astype(BF16)
        query_ref[...] = out[:, :HD]
        keyval_ref[...] = out[:, HD:]

    whole = lambda *shape: pl.BlockSpec(shape, lambda i: (0, 0))
    return pl.pallas_call(
        body,
        grid=(1,),
        in_specs=[whole(rows, width)] * BREADTH + [whole(width, 3 * HD)],
        out_specs=[whole(BREADTH * rows, HD), whole(BREADTH * rows, 2 * HD)],
        out_shape=[
            jax.ShapeDtypeStruct((BREADTH * rows, HD), BF16),
            jax.ShapeDtypeStruct((BREADTH * rows, 2 * HD), BF16),
        ],
        compiler_params=params(48),
        cost_estimate=cost(0, 0),
    )(*normed, weight)


def self_attention(spot, rows, queries, mine, other, weight):
    total_rows, width = queries.shape
    count = mine.shape[0]
    features = weight.shape[0]

    def index(n, x, core):
        at_z, at_x = n // total_rows, (x + BREADTH - (n // rows) % BREADTH) % BREADTH
        return ((at_z * BREADTH + at_x) * CORES + core) * rows + n % rows

    def body(spot_ref, q_ref, mine_ref, other_ref, weight_ref, *out_refs):
        z, x, core = spot_ref[0], spot_ref[1], spot_ref[2]
        n = lax.broadcasted_iota(jnp.int32, (1, count), 1)
        key = index(n, x, core)
        keys = (key, key + (1 - 2 * core) * rows)
        n = z * total_rows + lax.broadcasted_iota(jnp.int32, (total_rows, 1), 0)
        row = index(n, x, core)
        found = []
        for ref, key in zip((mine_ref, other_ref), keys):
            s = lax.dot_general(q_ref[...], ref[:, :width], NT, preferred_element_type=F32)
            found.append(jnp.where(key <= row, s * SCALE, NEG))
        peak = jnp.maximum(*[jnp.max(s, axis=1, keepdims=True) for s in found])
        total = jnp.zeros_like(peak)
        summed = jnp.zeros((total_rows, width), F32)
        for s, ref in zip(found, (mine_ref, other_ref)):
            weights = jnp.exp(s - peak)
            total = total + jnp.sum(weights, axis=1, keepdims=True)
            for part in split(weights):
                summed = summed + jnp.dot(part, ref[:, width:], preferred_element_type=F32)
        context = (summed / total).astype(BF16)
        out = lax.dot_general(context, weight_ref[...], NT, preferred_element_type=F32)
        out = out.astype(BF16)
        for k, ref in enumerate(out_refs):
            ref[...] = out[k * rows : (k + 1) * rows]

    whole = lambda *shape: pl.BlockSpec(shape, lambda i, p: (0, 0))
    return pl.pallas_call(
        body,
        grid_spec=pltpu.PrefetchScalarGridSpec(
            num_scalar_prefetch=1,
            grid=(1,),
            in_specs=[whole(total_rows, width)]
            + [whole(count, 2 * width)] * CORES
            + [whole(features, width)],
            out_specs=[whole(rows, features)] * BREADTH,
        ),
        out_shape=[jax.ShapeDtypeStruct((rows, features), BF16)] * BREADTH,
        compiler_params=params(48),
        cost_estimate=cost(0, 0),
    )(spot, queries, mine, other, weight)


def norm_own(index, base, terms, gain):
    rows, width = base.shape
    piece = width // TP

    def body(index_ref, base_ref, a, b, c, d, gain_ref, own_ref, normed_ref, total_ref):
        total, normed = add_and_norm(base_ref, (a, b, c, d), gain_ref)
        total_ref[...] = total
        normed_ref[...] = normed
        own_ref[...] = total_ref[:, pl.ds(pl.multiple_of(index_ref[0] * piece, piece), piece)]

    vmem = pl.BlockSpec(memory_space=pltpu.VMEM)
    return pl.pallas_call(
        body,
        in_specs=[pl.BlockSpec(memory_space=pltpu.SMEM)] + [vmem] * 6,
        out_specs=[vmem] * 2,
        out_shape=[
            jax.ShapeDtypeStruct((rows, piece), BF16),
            jax.ShapeDtypeStruct((rows, width), BF16),
        ],
        scratch_shapes=[pltpu.VMEM((rows, width), BF16)],
        compiler_params=params(),
        cost_estimate=cost(0, 0),
    )(index, base, *terms, gain)


def mlp(spot, normed, weight):
    rows, width = normed[0].shape
    share = weight.shape[-1] // 3
    piece = width // TP

    def body(spot_ref, *refs):
        rows_ref, out_ref, weight_ref, sems = refs[BREADTH:]
        start_copies(spot_ref[1], rows_ref, [weight_ref], sems)
        latents = jnp.concatenate([ref[...] for ref in refs[:BREADTH]], axis=0)
        wait_copies([weight_ref], sems)
        both = weight_ref[:, : 2 * share]
        both = jnp.dot(latents, both, preferred_element_type=F32)
        inner = (jax.nn.silu(both[:, :share]) * both[:, share:]).astype(BF16)
        for t in range(TP):
            term = lax.dot_general(
                inner,
                weight_ref[t * piece : (t + 1) * piece, 2 * share :],
                NT,
                preferred_element_type=F32,
            ).astype(BF16)
            for k in range(BREADTH):
                chip = lax.rem(spot_ref[1] + BREADTH - k, BREADTH)
                out_ref[chip * TP + t] = term[k * rows : (k + 1) * rows]

    vmem = pl.BlockSpec(memory_space=pltpu.VMEM)
    return pl.pallas_call(
        body,
        in_specs=[pl.BlockSpec(memory_space=pltpu.SMEM)]
        + [vmem] * BREADTH
        + [pl.BlockSpec(memory_space=pl.ANY)],
        out_specs=vmem,
        out_shape=jax.ShapeDtypeStruct((BREADTH * TP, rows, piece), BF16),
        scratch_shapes=[
            pltpu.VMEM((width, 3 * share), BF16),
            pltpu.SemaphoreType.DMA((1,)),
        ],
        compiler_params=params(58),
        cost_estimate=cost(0, 0),
    )(spot, *normed, weight)


def local(
    prefix,
    latent_in,
    latent_pos,
    w_query,
    w_keyval,
    w_cross_out,
    attn_gain,
    w_self_qkv,
    w_self_out,
    mlp_gain,
    w_gate_up,
    w_down,
):
    chips = lax.axis_size(ZX)
    core = lax.axis_index("core")
    tp = lax.axis_index("tp")
    rows = latent_in.shape[0]
    positions = prefix.shape[0]
    steps = jnp.arange(TP, dtype=jnp.int32)
    source = (tp - steps) % TP

    x = lax.axis_index("x")
    heads = pack(x.astype(jnp.int32)[None], w_self_qkv, w_self_out.T, w_gate_up, w_down.T)
    latent_pieces = everyone(latent_in)
    latent_pieces, heads = lax.optimization_barrier((latent_pieces, heads))
    beside = [shifted(heads[k + 1], "x", k, BREADTH) for k in range(1, BREADTH)]
    head_rows = jnp.stack([heads[0]] + [piece[:, : 4 * HD] for piece in beside])
    unit_rows = jnp.stack([heads[1]] + [piece[:, 4 * HD :] for piece in beside])

    prefix_pieces = everyone(prefix)
    queries, latents = project_queries(source, latent_pieces, w_query)
    queries, prefix_pieces, head_rows, unit_rows = lax.optimization_barrier(
        (queries, prefix_pieces, head_rows, unit_rows)
    )
    spread = jnp.broadcast_to(queries, (DEPTH, *queries.shape)).reshape(chips, rows, HD)
    all_queries = lax.all_to_all(spread, ZX, 0, 0).reshape(chips * rows, HD)
    head_rows = lax.all_gather(head_rows, ("z", "core"), axis=0)
    unit_rows = lax.all_gather(unit_rows, ("z", "core"), axis=0)

    keyval = project_keyval(jnp.concatenate([source, x[None]]), prefix_pieces, w_keyval)
    keyval = [keyval[0]] + [shifted(keyval[k], "x", k, BREADTH) for k in range(1, BREADTH)]
    keyval = keyval + [shifted(piece, "core", 1, CORES) for piece in keyval]
    z = lax.axis_index("z")
    beside = jnp.concatenate([(x - steps) % BREADTH] * CORES)
    at_core = jnp.repeat(jnp.stack([core, 1 - core]), BREADTH)
    bases = ((z * BREADTH + beside) * CORES + at_core).astype(jnp.int32) * positions
    pos = lax.dynamic_index_in_dim(
        latent_pos.reshape(chips, CORES, rows), core, axis=1, keepdims=False
    ).reshape(1, chips * rows)
    partial = cross_partial(bases, pos, all_queries, keyval)
    partial = lax.all_to_all(partial.reshape(chips, rows, -1), ZX, 0, 0)
    partial = partial.reshape(DEPTH, BREADTH, rows, -1)
    spot = jnp.stack([z, x, core]).astype(jnp.int32)
    split_cores = lambda x: x.reshape(DEPTH, CORES, *x.shape[1:])
    weights = assemble(spot, split_cores(head_rows), (3 * HD, HD))
    partial, weights = lax.optimization_barrier((partial, weights))
    w_qkv, w_out = weights
    cross_terms = combine_and_project(partial, w_cross_out)

    first, normed = norm(latents, everyone(cross_terms), attn_gain[None])
    group = [normed] + [shifted(normed, "x", k, BREADTH) for k in range(1, BREADTH)]
    queries, keyval = project_head(group, w_qkv)
    spread = jnp.broadcast_to(keyval, (DEPTH, *keyval.shape))
    mine = lax.all_to_all(spread, "z", 0, 0).reshape(-1, keyval.shape[1])
    other = shifted(mine, "core", 1, CORES)
    terms = self_attention(spot, rows, queries, mine, other, w_out)
    terms = [terms[0]] + [shifted(terms[k], "x", BREADTH - k, BREADTH) for k in range(1, BREADTH)]
    out_terms = sum(term.astype(F32) for term in terms).astype(BF16)

    own, normed = norm_own(tp.astype(jnp.int32)[None], first, everyone(out_terms), mlp_gain[None])
    group = [normed] + [shifted(normed, "x", k, BREADTH) for k in range(1, BREADTH)]
    down_terms = lax.all_to_all(mlp(spot, group, split_cores(unit_rows)), ("x", "tp"), 0, 0)
    return (own.astype(F32) + jnp.sum(down_terms.astype(F32), axis=0)).astype(BF16)


def solution(mesh):
    z, x, core, y = DEPTH, BREADTH, CORES, TP
    grid = Mesh(mesh.devices.reshape(z, x, core, y), ("z", "x", "core", "tp"))
    return jax.shard_map(
        local,
        mesh=grid,
        in_specs=(
            P(SEQ, "tp"),
            P(SEQ, "tp"),
            P(),
            P(None, "tp"),
            P(None, None, "tp"),
            P("tp", None),
            P(),
            P(None, SEQ, "tp"),
            P("tp", SEQ),
            P(),
            P(None, SEQ, "tp"),
            P("tp", SEQ),
        ),
        out_specs=P(SEQ, "tp"),
        check_vma=False,
    )
```

```python
import jax
import jax.numpy as jnp
from jax import lax
from jax.experimental import pallas as pl
from jax.experimental.pallas import tpu as pltpu
from jax.sharding import Mesh
from jax.sharding import PartitionSpec as P

HD = 128
NEG = -1e30
EPS = 1e-05
SCALE = HD ** (-0.5)
LOG2E = 1.4426950408889634
TP = 4
CORES = 2
DEPTH = 8
BREADTH = 4
LANES = 128
ZX = ("z", "x")
SEQ = ("z", "x", "core")
BF16 = jnp.bfloat16
F32 = jnp.float32
NT = (((1,), (1,)), ((), ()))
TN = (((0,), (0,)), ((), ()))


def shifted(x, axis, shift, count):
    return lax.ppermute(x, axis, [(i, (i + shift) % count) for i in range(count)])


def everyone(x):
    return [x] + [shifted(x, "tp", k, TP) for k in range(1, TP)]


def split(weights):
    high = weights.astype(BF16)
    low = (weights - high.astype(F32)).astype(BF16)
    return high, low


def three_terms(x):
    one = x.astype(BF16).astype(F32)
    two = (x - one).astype(BF16).astype(F32)
    three = (x - one - two).astype(BF16).astype(F32)
    return one, two, three


def params(mib=48):
    return pltpu.CompilerParams(vmem_limit_bytes=mib * 1024 * 1024)


def cost():
    return pl.CostEstimate(flops=1, bytes_accessed=1, transcendentals=0)


def behind(at, steps, count):
    return lax.rem(at + count - steps, count)


def project_gathered(pieces, used, weight, body, out_shape):
    first, last = used
    rows, width = last - first, pieces[0].shape[1]
    groups, _, cols = weight.shape

    def kernel(*refs):
        tp = lax.axis_index("tp")
        piece_refs, weight_ref = refs[:TP], refs[TP]
        out_refs = refs[TP + 1 : -5]
        own_ref, held_ref, acc_ref, own_sems, sems = refs[-5:]
        copies = {}
        for k in range(TP):
            copies[k] = pltpu.make_async_copy(
                piece_refs[k].at[pl.ds(first, rows), :], own_ref.at[k], own_sems.at[k]
            )
            copies[k].start()
            at = pl.ds(pl.multiple_of(behind(tp, k, TP) * width, width), width)
            for g in range(groups):
                copies[k, g] = pltpu.make_async_copy(
                    weight_ref.at[g, at, :], held_ref.at[k, g], sems.at[k, g]
                )
                copies[k, g].start()
        for k in range(TP):
            copies[k].wait()
            piece = own_ref[k]
            for g in range(groups):
                copies[k, g].wait()
                term = jnp.dot(piece, held_ref[k, g], preferred_element_type=F32)
                acc_ref[g] = term if k == 0 else acc_ref[g] + term
        body(own_ref, acc_ref, out_refs)

    vmem = pl.BlockSpec(memory_space=pltpu.VMEM)
    return pl.pallas_call(
        kernel,
        in_specs=[pl.BlockSpec(memory_space=pl.ANY)] * (TP + 1),
        out_specs=[vmem] * len(out_shape),
        out_shape=out_shape,
        scratch_shapes=[
            pltpu.VMEM((TP, rows, width), BF16),
            pltpu.VMEM((TP, groups, width, cols), BF16),
            pltpu.VMEM((groups, rows, cols), F32),
            pltpu.SemaphoreType.DMA((TP,)),
            pltpu.SemaphoreType.DMA((TP, groups)),
        ],
        compiler_params=params(58),
        cost_estimate=cost(),
    )(*pieces, weight)


def project_queries(pieces, used, weight):
    first, last = used
    rows, width = last - first, pieces[0].shape[1]
    heads = weight.shape[1] // HD

    def body(own_ref, acc_ref, out_refs):
        tp = lax.axis_index("tp")
        query_ref, whole_ref = out_refs
        for k in range(TP):
            at = behind(tp, k, TP)
            columns = pl.ds(pl.multiple_of(at * width, width), width)
            whole_ref[:, columns] = own_ref[k]
        for h in range(heads):
            query = acc_ref[0, :, h * HD : (h + 1) * HD].astype(BF16)
            for z in range(DEPTH):
                query_ref[z * heads + h] = query

    out_shape = [
        jax.ShapeDtypeStruct((DEPTH * heads, rows, HD), BF16),
        jax.ShapeDtypeStruct((rows, TP * width), BF16),
    ]
    return project_gathered(pieces, used, weight[None], body, out_shape)


def project_keyval(pieces, used, weight):
    rows = used[1] - used[0]
    groups, _, _ = weight.shape

    def body(own_ref, acc_ref, out_refs):
        x = lax.axis_index("x")
        for k, ref in enumerate(out_refs):
            head = lax.rem(x + k, BREADTH)
            columns = pl.ds(pl.multiple_of(head * HD, HD), HD)
            for g in range(groups):
                ref[g] = acc_ref[g, :, columns].astype(BF16)

    out_shape = [jax.ShapeDtypeStruct((groups, rows, HD), BF16)] * BREADTH
    return project_gathered(pieces, used, weight, body, out_shape)


def cross_partial(pos, queries, pieces):
    count = queries.shape[0]
    positions = pieces[0].shape[1]
    rows = 128

    def body(pos_ref, q_ref, *refs):
        piece_refs, out_ref, stat_ref = refs[: len(pieces)], refs[-2], refs[-1]
        z, x, core = [lax.axis_index(name) for name in SEQ]
        pos, q = pos_ref[...], q_ref[...]
        found = []
        for n, ref in enumerate(piece_refs):
            s = lax.dot_general(ref[0], q, NT, preferred_element_type=F32)
            at_core = core if n < BREADTH else 1 - core
            chip = z * BREADTH + behind(x, n % BREADTH, BREADTH)
            key = (chip * CORES + at_core) * positions
            key = key + lax.broadcasted_iota(jnp.int32, s.shape, 0)
            found.append(jnp.where(key <= pos, s, NEG))
        floor = jnp.full((1, rows), NEG * 0.5, F32)
        for s in found:
            floor = jnp.maximum(floor, jnp.max(s, axis=0, keepdims=True))
        total = jnp.zeros((1, rows), F32)
        summed = jnp.zeros((HD, rows), F32)
        for s, ref in zip(found, piece_refs):
            weights = jnp.exp2((s - floor) * (SCALE * LOG2E))
            total = total + jnp.sum(weights, axis=0, keepdims=True)
            for part in split(weights):
                summed = summed + lax.dot_general(ref[1], part, TN, preferred_element_type=F32)
        out_ref[:, :HD] = summed.T.astype(BF16)
        stat_ref[...] = jnp.zeros_like(stat_ref)
        for n, term in enumerate(three_terms(floor * SCALE) + three_terms(total)):
            stat_ref[n : n + 1, :] = term
        out_ref[:, HD:] = stat_ref[...].T.astype(BF16)

    return pl.pallas_call(
        body,
        grid=(count // rows,),
        in_specs=[
            pl.BlockSpec((1, rows), lambda r: (0, r)),
            pl.BlockSpec((rows, HD), lambda r: (r, 0)),
        ]
        + [pl.BlockSpec(piece.shape, lambda r: (0, 0, 0)) for piece in pieces],
        out_specs=pl.BlockSpec((rows, HD + LANES), lambda r: (r, 0)),
        scratch_shapes=[pltpu.VMEM((LANES, rows), F32)],
        out_shape=jax.ShapeDtypeStruct((count, HD + LANES), BF16),
        compiler_params=params(),
        cost_estimate=cost(),
    )(pos, queries, *pieces)


def combine_and_project(terms, weight):
    _, heads, rows, _ = terms.shape

    def body(x_ref, w_ref, out_ref, context_ref):
        for h in range(heads):
            stats = x_ref[:, h, :, HD:].astype(F32)
            field = [stats[:, :, n : n + 1] for n in range(6)]
            peak = field[0] + field[1] + field[2]
            factor = jnp.exp(peak - jnp.max(peak, axis=0, keepdims=True))
            total = jnp.sum(factor * (field[3] + field[4] + field[5]), axis=0)
            summed = jnp.sum(factor * x_ref[:, h, :, :HD].astype(F32), axis=0)
            context_ref[:, h * HD : (h + 1) * HD] = (summed / total).astype(BF16)
        out_ref[...] = jnp.dot(
            context_ref[...], w_ref[...], preferred_element_type=F32
        ).astype(BF16)

    return pl.pallas_call(
        body,
        out_shape=jax.ShapeDtypeStruct((rows, weight.shape[1]), BF16),
        scratch_shapes=[pltpu.VMEM((rows, heads * HD), BF16)],
        compiler_params=params(),
        cost_estimate=cost(),
    )(terms, weight)


def add_and_norm(base_ref, term_refs, gain_ref):
    a, b, c, d = [ref[...].astype(F32) for ref in term_refs]
    total = (base_ref[...].astype(F32) + ((a + c) + (b + d))).astype(BF16)
    x = total.astype(F32)
    scale = lax.rsqrt(jnp.mean(x * x, axis=-1, keepdims=True) + EPS)
    return total, (x * scale * gain_ref[...]).astype(BF16)


def norm(base, terms, gain):
    rows, width = base.shape

    def body(base_ref, a, b, c, d, gain_ref, total_ref, normed_ref):
        total, normed = add_and_norm(base_ref, (a, b, c, d), gain_ref)
        total_ref[...] = total
        normed_ref[...] = normed

    return pl.pallas_call(
        body,
        out_shape=[jax.ShapeDtypeStruct((rows, width), BF16)] * 2,
        compiler_params=params(),
        cost_estimate=cost(),
    )(base, *terms, gain)


def pack(prefix, latent_in, w_self_qkv, w_self_out, w_gate_up, w_down):
    groups, depth, _ = w_self_qkv.shape
    share = w_down.shape[1] // BREADTH
    positions, features = prefix.shape
    joined = positions + latent_in.shape[0]

    def body(prefix_ref, latent_ref, qkv_ref, out_ref, gate_up_ref, down_ref, *refs):
        joined_ref, head_ref, unit_ref, *refs = refs
        x = lax.axis_index("x")
        joined_ref[:positions] = prefix_ref[...]
        joined_ref[positions:] = latent_ref[...]
        for k in range(BREADTH):
            chip = lax.rem(x + k, BREADTH)
            head = pl.ds(pl.multiple_of(chip * HD, HD), HD)
            units = pl.ds(pl.multiple_of(chip * share, share), share)
            parts = [qkv_ref[g, :, head] for g in range(groups)] + [out_ref[:, head]]
            more = [gate_up_ref[g, :, units] for g in range(2)] + [down_ref[:, units]]
            if k == 0:
                head_ref[...] = jnp.concatenate(parts, axis=1)
                unit_ref[...] = jnp.concatenate(more, axis=1)
            else:
                refs[k - 1][...] = jnp.concatenate(parts + more, axis=1)

    vmem = pl.BlockSpec(memory_space=pltpu.VMEM)
    widths = (4 * HD, 3 * share) + (4 * HD + 3 * share,) * (BREADTH - 1)
    return pl.pallas_call(
        body,
        in_specs=[vmem] * 6,
        out_specs=[vmem] * (1 + len(widths)),
        out_shape=[jax.ShapeDtypeStruct((joined, features), BF16)]
        + [jax.ShapeDtypeStruct((depth, width), BF16) for width in widths],
        cost_estimate=cost(),
    )(prefix, latent_in, w_self_qkv, w_self_out, w_gate_up, w_down)


def start_copies(rows_ref, out_refs, sems):
    depth = rows_ref.shape[3]
    x = lax.axis_index("x")
    first = 0
    for n, out_ref in enumerate(out_refs):
        columns = pl.ds(first, out_ref.shape[1])
        first += out_ref.shape[1]
        for z in range(DEPTH):
            for core in range(CORES):
                for k in range(BREADTH):
                    chip = z * BREADTH + behind(x, k, BREADTH)
                    at = pl.multiple_of((chip * CORES + core) * depth, depth)
                    pltpu.make_async_copy(
                        rows_ref.at[z, core, k, :, columns],
                        out_ref.at[pl.ds(at, depth)],
                        sems.at[n],
                    ).start()


def wait_copies(out_ref, sem):
    pltpu.make_async_copy(out_ref, out_ref, sem).wait()


def assemble(rows, splits):
    def body(rows_ref, *refs):
        out_refs, sems = refs[:-1], refs[-1]
        start_copies(rows_ref, out_refs, sems)
        for n, out_ref in enumerate(out_refs):
            wait_copies(out_ref, sems.at[n])

    count = DEPTH * BREADTH * CORES * rows.shape[3]
    return pl.pallas_call(
        body,
        in_specs=[pl.BlockSpec(memory_space=pl.ANY)],
        out_specs=[pl.BlockSpec(memory_space=pltpu.VMEM)] * len(splits),
        out_shape=[jax.ShapeDtypeStruct((count, width), BF16) for width in splits],
        scratch_shapes=[pltpu.SemaphoreType.DMA((len(splits),))],
        compiler_params=params(58),
        cost_estimate=cost(),
    )(rows)


def project_head(normed, weight):
    rows, width = normed[0].shape

    def body(*refs):
        latents = jnp.concatenate([ref[...] for ref in refs[:BREADTH]], axis=0)
        weight_ref, query_ref, keyval_ref = refs[BREADTH:]
        out = jnp.dot(latents, weight_ref[...], preferred_element_type=F32).astype(BF16)
        query_ref[...] = out[:, :HD]
        for z in range(DEPTH):
            keyval_ref[z] = out[:, HD:]

    whole = lambda *shape: pl.BlockSpec(shape, lambda i: (0, 0))
    return pl.pallas_call(
        body,
        grid=(1,),
        in_specs=[whole(rows, width)] * BREADTH + [whole(width, 3 * HD)],
        out_specs=[
            whole(BREADTH * rows, HD),
            pl.BlockSpec((DEPTH, BREADTH * rows, 2 * HD), lambda i: (0, 0, 0)),
        ],
        out_shape=[
            jax.ShapeDtypeStruct((BREADTH * rows, HD), BF16),
            jax.ShapeDtypeStruct((DEPTH, BREADTH * rows, 2 * HD), BF16),
        ],
        compiler_params=params(48),
        cost_estimate=cost(),
    )(*normed, weight)


def self_attention(rows, queries, mine, other, weight):
    total_rows, width = queries.shape
    count = mine.shape[0]
    features = weight.shape[0]

    def index(n, x, core):
        at_z, at_x = n // total_rows, (x + BREADTH - (n // rows) % BREADTH) % BREADTH
        return ((at_z * BREADTH + at_x) * CORES + core) * rows + n % rows

    def body(q_ref, mine_ref, other_ref, weight_ref, *out_refs):
        z, x, core = [lax.axis_index(name) for name in SEQ]
        n = lax.broadcasted_iota(jnp.int32, (1, count), 1)
        key = index(n, x, core)
        keys = (key, key + (1 - 2 * core) * rows)
        n = z * total_rows + lax.broadcasted_iota(jnp.int32, (total_rows, 1), 0)
        row = index(n, x, core)
        found = []
        for ref, key in zip((mine_ref, other_ref), keys):
            s = lax.dot_general(q_ref[...], ref[:, :width], NT, preferred_element_type=F32)
            found.append(jnp.where(key <= row, s * SCALE, NEG))
        peak = jnp.maximum(*[jnp.max(s, axis=1, keepdims=True) for s in found])
        total = jnp.zeros_like(peak)
        summed = jnp.zeros((total_rows, width), F32)
        for s, ref in zip(found, (mine_ref, other_ref)):
            weights = jnp.exp(s - peak)
            total = total + jnp.sum(weights, axis=1, keepdims=True)
            for part in split(weights):
                summed = summed + jnp.dot(part, ref[:, width:], preferred_element_type=F32)
        context = (summed / total).astype(BF16)
        out = lax.dot_general(context, weight_ref[...], NT, preferred_element_type=F32)
        out = out.astype(BF16)
        for k, ref in enumerate(out_refs):
            ref[...] = out[k * rows : (k + 1) * rows]

    return pl.pallas_call(
        body,
        out_shape=[jax.ShapeDtypeStruct((rows, features), BF16)] * BREADTH,
        compiler_params=params(48),
        cost_estimate=cost(),
    )(queries, mine, other, weight)


def norm_own(base, terms, gain):
    rows, width = base.shape
    piece = width // TP

    def body(base_ref, a, b, c, d, gain_ref, own_ref, normed_ref, total_ref):
        tp = lax.axis_index("tp")
        total, normed = add_and_norm(base_ref, (a, b, c, d), gain_ref)
        total_ref[...] = total
        normed_ref[...] = normed
        own_ref[...] = total_ref[:, pl.ds(pl.multiple_of(tp * piece, piece), piece)]

    vmem = pl.BlockSpec(memory_space=pltpu.VMEM)
    return pl.pallas_call(
        body,
        in_specs=[vmem] * 6,
        out_specs=[vmem] * 2,
        out_shape=[
            jax.ShapeDtypeStruct((rows, piece), BF16),
            jax.ShapeDtypeStruct((rows, width), BF16),
        ],
        scratch_shapes=[pltpu.VMEM((rows, width), BF16)],
        compiler_params=params(),
        cost_estimate=cost(),
    )(base, *terms, gain)


def mlp(normed, weight):
    rows, width = normed[0].shape
    share = weight.shape[-1] // 3
    piece = width // TP

    def body(*refs):
        rows_ref, out_ref, both_ref, down_ref, sems = refs[BREADTH:]
        x = lax.axis_index("x")
        start_copies(rows_ref, (both_ref, down_ref), sems)
        latents = jnp.concatenate([ref[...] for ref in refs[:BREADTH]], axis=0)
        wait_copies(both_ref, sems.at[0])
        both = jnp.dot(latents, both_ref[...], preferred_element_type=F32)
        inner = (jax.nn.silu(both[:, :share]) * both[:, share:]).astype(BF16)
        wait_copies(down_ref, sems.at[1])
        for t in range(TP):
            term = lax.dot_general(
                inner,
                down_ref[t * piece : (t + 1) * piece, :],
                NT,
                preferred_element_type=F32,
            ).astype(BF16)
            for k in range(BREADTH):
                out_ref[behind(x, k, BREADTH) * TP + t] = term[k * rows : (k + 1) * rows]

    vmem = pl.BlockSpec(memory_space=pltpu.VMEM)
    return pl.pallas_call(
        body,
        in_specs=[vmem] * BREADTH
        + [pl.BlockSpec(memory_space=pl.ANY)],
        out_specs=vmem,
        out_shape=jax.ShapeDtypeStruct((BREADTH * TP, rows, piece), BF16),
        scratch_shapes=[
            pltpu.VMEM((width, 2 * share), BF16),
            pltpu.VMEM((width, share), BF16),
            pltpu.SemaphoreType.DMA((2,)),
        ],
        compiler_params=params(58),
        cost_estimate=cost(),
    )(*normed, weight)


def local(
    prefix,
    latent_in,
    latent_pos,
    w_query,
    w_keyval,
    w_cross_out,
    attn_gain,
    w_self_qkv,
    w_self_out,
    mlp_gain,
    w_gate_up,
    w_down,
):
    chips = lax.axis_size(ZX)
    core = lax.axis_index("core")
    rows = latent_in.shape[0]
    joined, *heads = pack(prefix, latent_in, w_self_qkv, w_self_out.T, w_gate_up, w_down.T)
    pieces = everyone(joined)
    positions = prefix.shape[0]
    beside = [shifted(heads[k + 1], "x", k, BREADTH) for k in range(1, BREADTH)]
    head_rows = jnp.stack([heads[0]] + [piece[:, : 4 * HD] for piece in beside])
    unit_rows = jnp.stack([heads[1]] + [piece[:, 4 * HD :] for piece in beside])

    used = (positions, positions + rows)
    queries, latents = project_queries( pieces, used, w_query)
    queries, pieces, head_rows = lax.optimization_barrier((queries, pieces, head_rows))
    all_queries = lax.all_to_all(queries, ZX, 0, 0).reshape(chips * rows, HD)
    head_rows = lax.all_gather(head_rows, ("z", "core"), axis=0)

    keyval = project_keyval( pieces, (0, positions), w_keyval)
    keyval = [keyval[0]] + [shifted(keyval[k], "x", k, BREADTH) for k in range(1, BREADTH)]
    keyval = keyval + [shifted(piece, "core", 1, CORES) for piece in keyval]
    pos = lax.dynamic_index_in_dim(
        latent_pos.reshape(chips, CORES, rows), core, axis=1, keepdims=False
    ).reshape(1, chips * rows)
    partial = cross_partial(pos, all_queries, keyval)
    partial = lax.all_to_all(partial.reshape(chips, rows, -1), ZX, 0, 0)
    partial = partial.reshape(DEPTH, BREADTH, rows, -1)
    split_cores = lambda x: x.reshape(DEPTH, CORES, *x.shape[1:])
    weights = assemble(split_cores(head_rows), (3 * HD, HD))
    partial, weights, unit_rows = lax.optimization_barrier((partial, weights, unit_rows))
    unit_rows = lax.all_gather(unit_rows, ("z", "core"), axis=0)
    w_qkv, w_out = weights
    cross_terms = combine_and_project(partial, w_cross_out)

    first, normed = norm(latents, everyone(cross_terms), attn_gain[None])
    group = [normed] + [shifted(normed, "x", k, BREADTH) for k in range(1, BREADTH)]
    queries, keyval = project_head(group, w_qkv)
    mine = lax.all_to_all(keyval, "z", 0, 0).reshape(-1, keyval.shape[2])
    other = shifted(mine, "core", 1, CORES)
    terms = self_attention(rows, queries, mine, other, w_out)
    terms = [terms[0]] + [shifted(terms[k], "x", BREADTH - k, BREADTH) for k in range(1, BREADTH)]
    out_terms = sum(term.astype(F32) for term in terms).astype(BF16)

    own, normed = norm_own(first, everyone(out_terms), mlp_gain[None])
    group = [normed] + [shifted(normed, "x", k, BREADTH) for k in range(1, BREADTH)]
    down_terms = lax.all_to_all(mlp(group, split_cores(unit_rows)), ("x", "tp"), 0, 0)
    return (own.astype(F32) + jnp.sum(down_terms.astype(F32), axis=0)).astype(BF16)


def solution(mesh):
    z, x, core, y = DEPTH, BREADTH, CORES, TP
    grid = Mesh(mesh.devices.reshape(z, x, core, y), ("z", "x", "core", "tp"))
    return jax.shard_map(
        local,
        mesh=grid,
        in_specs=(
            P(SEQ, "tp"),
            P(SEQ, "tp"),
            P(),
            P(None, "tp"),
            P(None, None, "tp"),
            P("tp", None),
            P(),
            P(None, SEQ, "tp"),
            P("tp", SEQ),
            P(),
            P(None, SEQ, "tp"),
            P("tp", SEQ),
        ),
        out_specs=P(SEQ, "tp"),
        check_vma=False,
    )
```

```python
import jax
import jax.numpy as jnp
from jax import lax
from jax.experimental import pallas as pl
from jax.experimental.pallas import tpu as pltpu
from jax.sharding import Mesh
from jax.sharding import PartitionSpec as P

HD = 128
NEG = -1e30
EPS = 1e-05
SCALE = HD ** (-0.5)
LOG2E = 1.4426950408889634
TP = 4
CORES = 2
DEPTH = 8
BREADTH = 4
LANES = 128
ZX = ("z", "x")
SEQ = ("z", "x", "core")
BF16 = jnp.bfloat16
F32 = jnp.float32
NT = (((1,), (1,)), ((), ()))
TN = (((0,), (0,)), ((), ()))


def shifted(x, axis, shift, count):
    return lax.ppermute(x, axis, [(i, (i + shift) % count) for i in range(count)])


def everyone(x):
    return [x] + [shifted(x, "tp", k, TP) for k in range(1, TP)]


def split(weights):
    high = weights.astype(BF16)
    low = (weights - high.astype(F32)).astype(BF16)
    return high, low


def three_terms(x):
    one = x.astype(BF16).astype(F32)
    two = (x - one).astype(BF16).astype(F32)
    three = (x - one - two).astype(BF16).astype(F32)
    return one, two, three


def params(mib=48):
    return pltpu.CompilerParams(vmem_limit_bytes=mib * 1024 * 1024)


def cost():
    return pl.CostEstimate(flops=1, bytes_accessed=1, transcendentals=0)


def behind(at, steps, count):
    return lax.rem(at + count - steps, count)


def project_gathered(pieces, positions, w_query, w_keyval):
    total, width = pieces[0].shape
    rows = total - positions
    groups, _, cols = w_keyval.shape
    heads = cols // HD

    def body(*refs):
        piece_refs, query_weight_ref, keyval_weight_ref = refs[:TP], refs[TP], refs[TP + 1]
        query_ref, whole_ref, *keyval_refs = refs[TP + 2 : -8]
        own_ref, held_query_ref, held_keyval_ref, acc_query_ref, acc_keyval_ref = refs[-8:-3]
        own_sems, query_sems, keyval_sems = refs[-3:]
        x, tp = lax.axis_index("x"), lax.axis_index("tp")
        columns = [
            pl.ds(pl.multiple_of(behind(tp, k, TP) * width, width), width) for k in range(TP)
        ]
        own, query, keyval = {}, {}, {}
        for k in range(TP):
            own[k] = pltpu.make_async_copy(piece_refs[k], own_ref.at[k], own_sems.at[k])
            own[k].start()
            for g in range(groups):
                keyval[k, g] = pltpu.make_async_copy(
                    keyval_weight_ref.at[g, columns[k], :],
                    held_keyval_ref.at[k, g],
                    keyval_sems.at[k, g],
                )
                keyval[k, g].start()
        for k in range(TP):
            query[k] = pltpu.make_async_copy(
                query_weight_ref.at[columns[k], :], held_query_ref.at[k], query_sems.at[k]
            )
            query[k].start()
        for k in range(TP):
            own[k].wait()
            piece = own_ref[k, :positions, :]
            for g in range(groups):
                keyval[k, g].wait()
                term = jnp.dot(piece, held_keyval_ref[k, g], preferred_element_type=F32)
                acc_keyval_ref[g] = term if k == 0 else acc_keyval_ref[g] + term
        for k in range(TP):
            query[k].wait()
            piece = own_ref[k, positions:, :]
            whole_ref[:, columns[k]] = piece
            term = jnp.dot(piece, held_query_ref[k], preferred_element_type=F32)
            acc_query_ref[...] = term if k == 0 else acc_query_ref[...] + term
        for k, ref in enumerate(keyval_refs):
            head = pl.multiple_of(lax.rem(x + k, BREADTH) * HD, HD)
            for g in range(groups):
                ref[g] = acc_keyval_ref[g, :, pl.ds(head, HD)].astype(BF16)
        for h in range(heads):
            part = acc_query_ref[:, h * HD : (h + 1) * HD].astype(BF16)
            for z in range(DEPTH):
                query_ref[z * heads + h] = part

    vmem = pl.BlockSpec(memory_space=pltpu.VMEM)
    out_shape = [
        jax.ShapeDtypeStruct((DEPTH * heads, rows, HD), BF16),
        jax.ShapeDtypeStruct((rows, TP * width), BF16),
    ] + [jax.ShapeDtypeStruct((groups, positions, HD), BF16)] * BREADTH
    return pl.pallas_call(
        body,
        in_specs=[pl.BlockSpec(memory_space=pl.ANY)] * (TP + 2),
        out_specs=[vmem] * len(out_shape),
        out_shape=out_shape,
        scratch_shapes=[
            pltpu.VMEM((TP, total, width), BF16),
            pltpu.VMEM((TP, width, cols), BF16),
            pltpu.VMEM((TP, groups, width, cols), BF16),
            pltpu.VMEM((rows, cols), F32),
            pltpu.VMEM((groups, positions, cols), F32),
            pltpu.SemaphoreType.DMA((TP,)),
            pltpu.SemaphoreType.DMA((TP,)),
            pltpu.SemaphoreType.DMA((TP, groups)),
        ],
        compiler_params=params(58),
        cost_estimate=cost(),
    )(*pieces, w_query, w_keyval)


def cross_partial(pos, queries, pieces):
    count = queries.shape[0]
    positions = pieces[0].shape[1]
    rows = 128

    def body(pos_ref, q_ref, *refs):
        piece_refs, out_ref, stat_ref = refs[: len(pieces)], refs[-2], refs[-1]
        z, x, core = [lax.axis_index(name) for name in SEQ]
        pos, q = pos_ref[...], q_ref[...]
        found = []
        for n, ref in enumerate(piece_refs):
            s = lax.dot_general(ref[0], q, NT, preferred_element_type=F32)
            at_core = core if n < BREADTH else 1 - core
            chip = z * BREADTH + behind(x, n % BREADTH, BREADTH)
            key = (chip * CORES + at_core) * positions
            key = key + lax.broadcasted_iota(jnp.int32, s.shape, 0)
            found.append(jnp.where(key <= pos, s, NEG))
        floor = jnp.full((1, rows), NEG * 0.5, F32)
        for s in found:
            floor = jnp.maximum(floor, jnp.max(s, axis=0, keepdims=True))
        total = jnp.zeros((1, rows), F32)
        summed = jnp.zeros((HD, rows), F32)
        for s, ref in zip(found, piece_refs):
            weights = jnp.exp2((s - floor) * (SCALE * LOG2E))
            total = total + jnp.sum(weights, axis=0, keepdims=True)
            for part in split(weights):
                summed = summed + lax.dot_general(ref[1], part, TN, preferred_element_type=F32)
        out_ref[:, :HD] = summed.T.astype(BF16)
        stat_ref[...] = jnp.zeros_like(stat_ref)
        for n, term in enumerate(three_terms(floor * SCALE) + three_terms(total)):
            stat_ref[n : n + 1, :] = term
        out_ref[:, HD:] = stat_ref[...].T.astype(BF16)

    return pl.pallas_call(
        body,
        grid=(count // rows,),
        in_specs=[
            pl.BlockSpec((1, rows), lambda r: (0, r)),
            pl.BlockSpec((rows, HD), lambda r: (r, 0)),
        ]
        + [pl.BlockSpec(piece.shape, lambda r: (0, 0, 0)) for piece in pieces],
        out_specs=pl.BlockSpec((rows, HD + LANES), lambda r: (r, 0)),
        scratch_shapes=[pltpu.VMEM((LANES, rows), F32)],
        out_shape=jax.ShapeDtypeStruct((count, HD + LANES), BF16),
        compiler_params=params(),
        cost_estimate=cost(),
    )(pos, queries, *pieces)


def combine_and_project(terms, weight):
    _, heads, rows, _ = terms.shape

    def body(x_ref, w_ref, out_ref, context_ref):
        for h in range(heads):
            stats = x_ref[:, h, :, HD:].astype(F32)
            field = [stats[:, :, n : n + 1] for n in range(6)]
            peak = field[0] + field[1] + field[2]
            factor = jnp.exp(peak - jnp.max(peak, axis=0, keepdims=True))
            total = jnp.sum(factor * (field[3] + field[4] + field[5]), axis=0)
            summed = jnp.sum(factor * x_ref[:, h, :, :HD].astype(F32), axis=0)
            context_ref[:, h * HD : (h + 1) * HD] = (summed / total).astype(BF16)
        out_ref[...] = jnp.dot(
            context_ref[...], w_ref[...], preferred_element_type=F32
        ).astype(BF16)

    return pl.pallas_call(
        body,
        out_shape=jax.ShapeDtypeStruct((rows, weight.shape[1]), BF16),
        scratch_shapes=[pltpu.VMEM((rows, heads * HD), BF16)],
        compiler_params=params(),
        cost_estimate=cost(),
    )(terms, weight)


def add_and_norm(base_ref, term_refs, gain_ref):
    a, b, c, d = [ref[...].astype(F32) for ref in term_refs]
    total = (base_ref[...].astype(F32) + ((a + c) + (b + d))).astype(BF16)
    x = total.astype(F32)
    scale = lax.rsqrt(jnp.mean(x * x, axis=-1, keepdims=True) + EPS)
    return total, (x * scale * gain_ref[...]).astype(BF16)


def norm(base, terms, gain):
    rows, width = base.shape

    def body(base_ref, a, b, c, d, gain_ref, total_ref, normed_ref):
        total, normed = add_and_norm(base_ref, (a, b, c, d), gain_ref)
        total_ref[...] = total
        normed_ref[...] = normed

    return pl.pallas_call(
        body,
        out_shape=[jax.ShapeDtypeStruct((rows, width), BF16)] * 2,
        compiler_params=params(),
        cost_estimate=cost(),
    )(base, *terms, gain)


def pack(prefix, latent_in, w_self_qkv, w_self_out, w_gate_up, w_down):
    groups, depth, _ = w_self_qkv.shape
    share = w_down.shape[1] // BREADTH
    positions, features = prefix.shape
    joined = positions + latent_in.shape[0]

    def body(prefix_ref, latent_ref, qkv_ref, out_ref, gate_up_ref, down_ref, *refs):
        joined_ref, head_ref, unit_ref, *refs = refs
        x = lax.axis_index("x")
        joined_ref[:positions] = prefix_ref[...]
        joined_ref[positions:] = latent_ref[...]
        for k in range(BREADTH):
            chip = lax.rem(x + k, BREADTH)
            head = pl.ds(pl.multiple_of(chip * HD, HD), HD)
            units = pl.ds(pl.multiple_of(chip * share, share), share)
            parts = [qkv_ref[g, :, head] for g in range(groups)] + [out_ref[:, head]]
            more = [gate_up_ref[g, :, units] for g in range(2)] + [down_ref[:, units]]
            if k == 0:
                head_ref[...] = jnp.concatenate(parts, axis=1)
                unit_ref[...] = jnp.concatenate(more, axis=1)
            else:
                refs[k - 1][...] = jnp.concatenate(parts + more, axis=1)

    vmem = pl.BlockSpec(memory_space=pltpu.VMEM)
    widths = (4 * HD, 3 * share) + (4 * HD + 3 * share,) * (BREADTH - 1)
    return pl.pallas_call(
        body,
        in_specs=[vmem] * 6,
        out_specs=[vmem] * (1 + len(widths)),
        out_shape=[jax.ShapeDtypeStruct((joined, features), BF16)]
        + [jax.ShapeDtypeStruct((depth, width), BF16) for width in widths],
        compiler_params=params(58),
        cost_estimate=cost(),
    )(prefix, latent_in, w_self_qkv, w_self_out, w_gate_up, w_down)


def start_copies(rows_ref, out_refs, sems):
    depth = rows_ref.shape[3]
    x = lax.axis_index("x")
    first = 0
    for n, out_ref in enumerate(out_refs):
        columns = pl.ds(first, out_ref.shape[1])
        first += out_ref.shape[1]
        for z in range(DEPTH):
            for core in range(CORES):
                for k in range(BREADTH):
                    chip = z * BREADTH + behind(x, k, BREADTH)
                    at = pl.multiple_of((chip * CORES + core) * depth, depth)
                    pltpu.make_async_copy(
                        rows_ref.at[z, core, k, :, columns],
                        out_ref.at[pl.ds(at, depth)],
                        sems.at[n],
                    ).start()


def wait_copies(out_ref, sem):
    pltpu.make_async_copy(out_ref, out_ref, sem).wait()


def assemble(rows, splits):
    def body(rows_ref, *refs):
        out_refs, sems = refs[:-1], refs[-1]
        start_copies(rows_ref, out_refs, sems)
        for n, out_ref in enumerate(out_refs):
            wait_copies(out_ref, sems.at[n])

    count = DEPTH * BREADTH * CORES * rows.shape[3]
    return pl.pallas_call(
        body,
        in_specs=[pl.BlockSpec(memory_space=pl.ANY)],
        out_specs=[pl.BlockSpec(memory_space=pltpu.VMEM)] * len(splits),
        out_shape=[jax.ShapeDtypeStruct((count, width), BF16) for width in splits],
        scratch_shapes=[pltpu.SemaphoreType.DMA((len(splits),))],
        compiler_params=params(58),
        cost_estimate=cost(),
    )(rows)


def project_head(normed, weight):
    rows, width = normed[0].shape

    def body(*refs):
        latents = jnp.concatenate([ref[...] for ref in refs[:BREADTH]], axis=0)
        weight_ref, query_ref, keyval_ref = refs[BREADTH:]
        out = jnp.dot(latents, weight_ref[...], preferred_element_type=F32).astype(BF16)
        query_ref[...] = out[:, :HD]
        for z in range(DEPTH):
            keyval_ref[z] = out[:, HD:]

    whole = lambda *shape: pl.BlockSpec(shape, lambda i: (0, 0))
    return pl.pallas_call(
        body,
        grid=(1,),
        in_specs=[whole(rows, width)] * BREADTH + [whole(width, 3 * HD)],
        out_specs=[
            whole(BREADTH * rows, HD),
            pl.BlockSpec((DEPTH, BREADTH * rows, 2 * HD), lambda i: (0, 0, 0)),
        ],
        out_shape=[
            jax.ShapeDtypeStruct((BREADTH * rows, HD), BF16),
            jax.ShapeDtypeStruct((DEPTH, BREADTH * rows, 2 * HD), BF16),
        ],
        compiler_params=params(48),
        cost_estimate=cost(),
    )(*normed, weight)


def self_attention(rows, queries, mine, other, weight):
    total_rows, width = queries.shape
    count = mine.shape[0]
    features = weight.shape[0]

    def index(n, x, core):
        at_z, at_x = n // total_rows, (x + BREADTH - (n // rows) % BREADTH) % BREADTH
        return ((at_z * BREADTH + at_x) * CORES + core) * rows + n % rows

    def body(q_ref, mine_ref, other_ref, weight_ref, *out_refs):
        z, x, core = [lax.axis_index(name) for name in SEQ]
        n = lax.broadcasted_iota(jnp.int32, (1, count), 1)
        key = index(n, x, core)
        keys = (key, key + (1 - 2 * core) * rows)
        n = z * total_rows + lax.broadcasted_iota(jnp.int32, (total_rows, 1), 0)
        row = index(n, x, core)
        found = []
        for ref, key in zip((mine_ref, other_ref), keys):
            s = lax.dot_general(q_ref[...], ref[:, :width], NT, preferred_element_type=F32)
            found.append(jnp.where(key <= row, s * SCALE, NEG))
        peak = jnp.maximum(*[jnp.max(s, axis=1, keepdims=True) for s in found])
        total = jnp.zeros_like(peak)
        summed = jnp.zeros((total_rows, width), F32)
        for s, ref in zip(found, (mine_ref, other_ref)):
            weights = jnp.exp(s - peak)
            total = total + jnp.sum(weights, axis=1, keepdims=True)
            for part in split(weights):
                summed = summed + jnp.dot(part, ref[:, width:], preferred_element_type=F32)
        context = (summed / total).astype(BF16)
        out = lax.dot_general(context, weight_ref[...], NT, preferred_element_type=F32)
        out = out.astype(BF16)
        for k, ref in enumerate(out_refs):
            ref[...] = out[k * rows : (k + 1) * rows]

    return pl.pallas_call(
        body,
        out_shape=[jax.ShapeDtypeStruct((rows, features), BF16)] * BREADTH,
        compiler_params=params(48),
        cost_estimate=cost(),
    )(queries, mine, other, weight)


def norm_own(base, terms, gain):
    rows, width = base.shape
    piece = width // TP

    def body(base_ref, a, b, c, d, gain_ref, own_ref, normed_ref, total_ref):
        tp = lax.axis_index("tp")
        total, normed = add_and_norm(base_ref, (a, b, c, d), gain_ref)
        total_ref[...] = total
        normed_ref[...] = normed
        own_ref[...] = total_ref[:, pl.ds(pl.multiple_of(tp * piece, piece), piece)]

    vmem = pl.BlockSpec(memory_space=pltpu.VMEM)
    return pl.pallas_call(
        body,
        in_specs=[vmem] * 6,
        out_specs=[vmem] * 2,
        out_shape=[
            jax.ShapeDtypeStruct((rows, piece), BF16),
            jax.ShapeDtypeStruct((rows, width), BF16),
        ],
        scratch_shapes=[pltpu.VMEM((rows, width), BF16)],
        compiler_params=params(),
        cost_estimate=cost(),
    )(base, *terms, gain)


def mlp(normed, weight):
    rows, width = normed[0].shape
    share = weight.shape[-1] // 3
    piece = width // TP

    def body(*refs):
        rows_ref, out_ref, both_ref, down_ref, sems = refs[BREADTH:]
        x = lax.axis_index("x")
        start_copies(rows_ref, (both_ref, down_ref), sems)
        latents = jnp.concatenate([ref[...] for ref in refs[:BREADTH]], axis=0)
        wait_copies(both_ref, sems.at[0])
        both = jnp.dot(latents, both_ref[...], preferred_element_type=F32)
        inner = (jax.nn.silu(both[:, :share]) * both[:, share:]).astype(BF16)
        wait_copies(down_ref, sems.at[1])
        for t in range(TP):
            term = lax.dot_general(
                inner,
                down_ref[t * piece : (t + 1) * piece, :],
                NT,
                preferred_element_type=F32,
            ).astype(BF16)
            for k in range(BREADTH):
                out_ref[behind(x, k, BREADTH) * TP + t] = term[k * rows : (k + 1) * rows]

    vmem = pl.BlockSpec(memory_space=pltpu.VMEM)
    return pl.pallas_call(
        body,
        in_specs=[vmem] * BREADTH
        + [pl.BlockSpec(memory_space=pl.ANY)],
        out_specs=vmem,
        out_shape=jax.ShapeDtypeStruct((BREADTH * TP, rows, piece), BF16),
        scratch_shapes=[
            pltpu.VMEM((width, 2 * share), BF16),
            pltpu.VMEM((width, share), BF16),
            pltpu.SemaphoreType.DMA((2,)),
        ],
        compiler_params=params(32),
        cost_estimate=cost(),
    )(*normed, weight)


def local(
    prefix,
    latent_in,
    latent_pos,
    w_query,
    w_keyval,
    w_cross_out,
    attn_gain,
    w_self_qkv,
    w_self_out,
    mlp_gain,
    w_gate_up,
    w_down,
):
    chips = lax.axis_size(ZX)
    core = lax.axis_index("core")
    rows = latent_in.shape[0]
    joined, *heads = pack(prefix, latent_in, w_self_qkv, w_self_out.T, w_gate_up, w_down.T)
    pieces = everyone(joined)
    positions = prefix.shape[0]
    beside = [shifted(heads[k + 1], "x", k, BREADTH) for k in range(1, BREADTH)]
    head_rows = jnp.stack([heads[0]] + [piece[:, : 4 * HD] for piece in beside])
    unit_rows = jnp.stack([heads[1]] + [piece[:, 4 * HD :] for piece in beside])

    pieces, head_rows = lax.optimization_barrier((pieces, head_rows))
    queries, latents, *keyval = project_gathered(pieces, positions, w_query, w_keyval)
    all_queries = lax.all_to_all(queries, ZX, 0, 0).reshape(chips * rows, HD)
    head_rows = lax.all_gather(head_rows, ("z", "core"), axis=0)

    keyval = [keyval[0]] + [shifted(keyval[k], "x", k, BREADTH) for k in range(1, BREADTH)]
    keyval = keyval + [shifted(piece, "core", 1, CORES) for piece in keyval]
    pos = lax.dynamic_index_in_dim(
        latent_pos.reshape(chips, CORES, rows), core, axis=1, keepdims=False
    ).reshape(1, chips * rows)
    partial = cross_partial(pos, all_queries, keyval)
    partial = lax.all_to_all(partial.reshape(chips, rows, -1), ZX, 0, 0)
    partial = partial.reshape(DEPTH, BREADTH, rows, -1)
    split_cores = lambda x: x.reshape(DEPTH, CORES, *x.shape[1:])
    weights = assemble(split_cores(head_rows), (3 * HD, HD))
    partial, weights, unit_rows = lax.optimization_barrier((partial, weights, unit_rows))
    unit_rows = lax.all_gather(unit_rows, ("z", "core"), axis=0)
    w_qkv, w_out = weights
    cross_terms = combine_and_project(partial, w_cross_out)

    first, normed = norm(latents, everyone(cross_terms), attn_gain[None])
    group = [normed] + [shifted(normed, "x", k, BREADTH) for k in range(1, BREADTH)]
    queries, keyval = project_head(group, w_qkv)
    mine = lax.all_to_all(keyval, "z", 0, 0).reshape(-1, keyval.shape[2])
    other = shifted(mine, "core", 1, CORES)
    terms = self_attention(rows, queries, mine, other, w_out)
    terms = [terms[0]] + [shifted(terms[k], "x", BREADTH - k, BREADTH) for k in range(1, BREADTH)]
    out_terms = sum(term.astype(F32) for term in terms).astype(BF16)

    own, normed = norm_own(first, everyone(out_terms), mlp_gain[None])
    group = [normed] + [shifted(normed, "x", k, BREADTH) for k in range(1, BREADTH)]
    down_terms = lax.all_to_all(mlp(group, split_cores(unit_rows)), ("x", "tp"), 0, 0)
    return (own.astype(F32) + jnp.sum(down_terms.astype(F32), axis=0)).astype(BF16)


def solution(mesh):
    z, x, core, y = DEPTH, BREADTH, CORES, TP
    grid = Mesh(mesh.devices.reshape(z, x, core, y), ("z", "x", "core", "tp"))
    return jax.shard_map(
        local,
        mesh=grid,
        in_specs=(
            P(SEQ, "tp"),
            P(SEQ, "tp"),
            P(),
            P(None, "tp"),
            P(None, None, "tp"),
            P("tp", None),
            P(),
            P(None, SEQ, "tp"),
            P("tp", SEQ),
            P(),
            P(None, SEQ, "tp"),
            P("tp", SEQ),
        ),
        out_specs=P(SEQ, "tp"),
        check_vma=False,
    )
```

```python
import jax
import jax.numpy as jnp
from jax import lax
from jax.experimental import pallas as pl
from jax.experimental.pallas import tpu as pltpu
from jax.sharding import Mesh
from jax.sharding import PartitionSpec as P

HD = 128
NEG = -1e30
EPS = 1e-05
SCALE = HD ** (-0.5)
LOG2E = 1.4426950408889634
TP = 4
CORES = 2
DEPTH = 8
BREADTH = 4
LANES = 128
ZX = ("z", "x")
SEQ = ("z", "x", "core")
BF16 = jnp.bfloat16
F32 = jnp.float32
NT = (((1,), (1,)), ((), ()))
TN = (((0,), (0,)), ((), ()))


def shifted(x, axis, shift, count):
    return lax.ppermute(x, axis, [(i, (i + shift) % count) for i in range(count)])


def everyone(x):
    return [x] + [shifted(x, "tp", k, TP) for k in range(1, TP)]


def split(weights):
    high = weights.astype(BF16)
    low = (weights - high.astype(F32)).astype(BF16)
    return high, low


def three_terms(x):
    one = x.astype(BF16).astype(F32)
    two = (x - one).astype(BF16).astype(F32)
    three = (x - one - two).astype(BF16).astype(F32)
    return one, two, three


def params(mib=48):
    return pltpu.CompilerParams(vmem_limit_bytes=mib * 1024 * 1024)


def cost():
    return pl.CostEstimate(flops=1, bytes_accessed=1, transcendentals=0)


def behind(at, steps, count):
    return lax.rem(at + count - steps, count)


def project_gathered(pieces, positions, w_query, w_keyval):
    total, width = pieces[0].shape
    rows = total - positions
    groups, _, cols = w_keyval.shape
    heads = cols // HD

    def body(*refs):
        piece_refs, query_weight_ref, keyval_weight_ref = refs[:TP], refs[TP], refs[TP + 1]
        query_ref, whole_ref, *keyval_refs = refs[TP + 2 : -8]
        own_ref, held_query_ref, held_keyval_ref, acc_query_ref, acc_keyval_ref = refs[-8:-3]
        own_sems, query_sems, keyval_sems = refs[-3:]
        x, tp = lax.axis_index("x"), lax.axis_index("tp")
        columns = [
            pl.ds(pl.multiple_of(behind(tp, k, TP) * width, width), width) for k in range(TP)
        ]
        own, query, keyval = {}, {}, {}
        for k in range(TP):
            own[k] = pltpu.make_async_copy(piece_refs[k], own_ref.at[k], own_sems.at[k])
            own[k].start()
            for g in range(groups):
                keyval[k, g] = pltpu.make_async_copy(
                    keyval_weight_ref.at[g, columns[k], :],
                    held_keyval_ref.at[k, g],
                    keyval_sems.at[k, g],
                )
                keyval[k, g].start()
        for k in range(TP):
            query[k] = pltpu.make_async_copy(
                query_weight_ref.at[columns[k], :], held_query_ref.at[k], query_sems.at[k]
            )
            query[k].start()
        for k in range(TP):
            own[k].wait()
            piece = own_ref[k, :positions, :]
            for g in range(groups):
                keyval[k, g].wait()
                term = jnp.dot(piece, held_keyval_ref[k, g], preferred_element_type=F32)
                acc_keyval_ref[g] = term if k == 0 else acc_keyval_ref[g] + term
        for k in range(TP):
            query[k].wait()
            piece = own_ref[k, positions:, :]
            whole_ref[:, columns[k]] = piece
            term = jnp.dot(piece, held_query_ref[k], preferred_element_type=F32)
            acc_query_ref[...] = term if k == 0 else acc_query_ref[...] + term
        for k, ref in enumerate(keyval_refs):
            head = pl.multiple_of(lax.rem(x + k, BREADTH) * HD, HD)
            for g in range(groups):
                ref[g] = acc_keyval_ref[g, :, pl.ds(head, HD)].astype(BF16)
        for h in range(heads):
            part = acc_query_ref[:, h * HD : (h + 1) * HD].astype(BF16)
            for z in range(DEPTH):
                query_ref[z * heads + h] = part

    vmem = pl.BlockSpec(memory_space=pltpu.VMEM)
    out_shape = [
        jax.ShapeDtypeStruct((DEPTH * heads, rows, HD), BF16),
        jax.ShapeDtypeStruct((rows, TP * width), BF16),
    ] + [jax.ShapeDtypeStruct((groups, positions, HD), BF16)] * BREADTH
    return pl.pallas_call(
        body,
        in_specs=[pl.BlockSpec(memory_space=pl.ANY)] * (TP + 2),
        out_specs=[vmem] * len(out_shape),
        out_shape=out_shape,
        scratch_shapes=[
            pltpu.VMEM((TP, total, width), BF16),
            pltpu.VMEM((TP, width, cols), BF16),
            pltpu.VMEM((TP, groups, width, cols), BF16),
            pltpu.VMEM((rows, cols), F32),
            pltpu.VMEM((groups, positions, cols), F32),
            pltpu.SemaphoreType.DMA((TP,)),
            pltpu.SemaphoreType.DMA((TP,)),
            pltpu.SemaphoreType.DMA((TP, groups)),
        ],
        compiler_params=params(58),
        cost_estimate=cost(),
    )(*pieces, w_query, w_keyval)


def cross_partial(pos, queries, pieces):
    count = queries.shape[0]
    positions = pieces[0].shape[1]
    rows = 256

    def body(pos_ref, q_ref, *refs):
        piece_refs, out_ref, stat_ref = refs[: len(pieces)], refs[-2], refs[-1]
        z, x, core = [lax.axis_index(name) for name in SEQ]
        pos, q = pos_ref[...], q_ref[...]
        found = []
        for n, ref in enumerate(piece_refs):
            s = lax.dot_general(ref[0], q, NT, preferred_element_type=F32)
            at_core = core if n < BREADTH else 1 - core
            chip = z * BREADTH + behind(x, n % BREADTH, BREADTH)
            key = (chip * CORES + at_core) * positions
            key = key + lax.broadcasted_iota(jnp.int32, s.shape, 0)
            found.append(jnp.where(key <= pos, s, NEG))
        floor = jnp.full((1, rows), NEG * 0.5, F32)
        for s in found:
            floor = jnp.maximum(floor, jnp.max(s, axis=0, keepdims=True))
        total = jnp.zeros((1, rows), F32)
        summed = jnp.zeros((HD, rows), F32)
        for s, ref in zip(found, piece_refs):
            weights = jnp.exp2((s - floor) * (SCALE * LOG2E))
            total = total + jnp.sum(weights, axis=0, keepdims=True)
            for part in split(weights):
                summed = summed + lax.dot_general(ref[1], part, TN, preferred_element_type=F32)
        out_ref[:, :HD] = summed.T.astype(BF16)
        stat_ref[...] = jnp.zeros_like(stat_ref)
        for n, term in enumerate(three_terms(floor * SCALE) + three_terms(total)):
            stat_ref[n : n + 1, :] = term
        out_ref[:, HD:] = stat_ref[...].T.astype(BF16)

    return pl.pallas_call(
        body,
        grid=(count // rows,),
        in_specs=[
            pl.BlockSpec((1, rows), lambda r: (0, r)),
            pl.BlockSpec((rows, HD), lambda r: (r, 0)),
        ]
        + [pl.BlockSpec(piece.shape, lambda r: (0, 0, 0)) for piece in pieces],
        out_specs=pl.BlockSpec((rows, HD + LANES), lambda r: (r, 0)),
        scratch_shapes=[pltpu.VMEM((LANES, rows), F32)],
        out_shape=jax.ShapeDtypeStruct((count, HD + LANES), BF16),
        compiler_params=params(),
        cost_estimate=cost(),
    )(pos, queries, *pieces)


def combine_and_project(terms, weight):
    _, heads, rows, _ = terms.shape

    def body(x_ref, w_ref, out_ref, context_ref):
        for h in range(heads):
            stats = x_ref[:, h, :, HD:].astype(F32)
            field = [stats[:, :, n : n + 1] for n in range(6)]
            peak = field[0] + field[1] + field[2]
            factor = jnp.exp(peak - jnp.max(peak, axis=0, keepdims=True))
            total = jnp.sum(factor * (field[3] + field[4] + field[5]), axis=0)
            summed = jnp.sum(factor * x_ref[:, h, :, :HD].astype(F32), axis=0)
            context_ref[:, h * HD : (h + 1) * HD] = (summed / total).astype(BF16)
        out_ref[...] = jnp.dot(
            context_ref[...], w_ref[...], preferred_element_type=F32
        ).astype(BF16)

    return pl.pallas_call(
        body,
        out_shape=jax.ShapeDtypeStruct((rows, weight.shape[1]), BF16),
        scratch_shapes=[pltpu.VMEM((rows, heads * HD), BF16)],
        compiler_params=params(),
        cost_estimate=cost(),
    )(terms, weight)


def add_and_norm(base_ref, term_refs, gain_ref):
    a, b, c, d = [ref[...].astype(F32) for ref in term_refs]
    total = (base_ref[...].astype(F32) + ((a + c) + (b + d))).astype(BF16)
    x = total.astype(F32)
    scale = lax.rsqrt(jnp.mean(x * x, axis=-1, keepdims=True) + EPS)
    return total, (x * scale * gain_ref[...]).astype(BF16)


def norm(base, terms, gain):
    rows, width = base.shape

    def body(base_ref, a, b, c, d, gain_ref, total_ref, normed_ref):
        total, normed = add_and_norm(base_ref, (a, b, c, d), gain_ref)
        total_ref[...] = total
        normed_ref[...] = normed

    return pl.pallas_call(
        body,
        out_shape=[jax.ShapeDtypeStruct((rows, width), BF16)] * 2,
        compiler_params=params(),
        cost_estimate=cost(),
    )(base, *terms, gain)


def pack(prefix, latent_in, w_self_qkv, w_self_out, w_gate_up, w_down):
    groups, depth, _ = w_self_qkv.shape
    share = w_down.shape[1] // BREADTH
    positions, features = prefix.shape
    joined = positions + latent_in.shape[0]

    def body(prefix_ref, latent_ref, qkv_ref, out_ref, gate_up_ref, down_ref, *refs):
        joined_ref, head_ref, unit_ref, *refs = refs
        x = lax.axis_index("x")
        joined_ref[:positions] = prefix_ref[...]
        joined_ref[positions:] = latent_ref[...]
        for k in range(BREADTH):
            chip = lax.rem(x + k, BREADTH)
            head = pl.ds(pl.multiple_of(chip * HD, HD), HD)
            units = pl.ds(pl.multiple_of(chip * share, share), share)
            parts = [qkv_ref[g, :, head] for g in range(groups)] + [out_ref[:, head]]
            more = [gate_up_ref[g, :, units] for g in range(2)] + [down_ref[:, units]]
            if k == 0:
                head_ref[...] = jnp.concatenate(parts, axis=1)
                unit_ref[...] = jnp.concatenate(more, axis=1)
            else:
                refs[k - 1][...] = jnp.concatenate(parts + more, axis=1)

    vmem = pl.BlockSpec(memory_space=pltpu.VMEM)
    widths = (4 * HD, 3 * share) + (4 * HD + 3 * share,) * (BREADTH - 1)
    return pl.pallas_call(
        body,
        in_specs=[vmem] * 6,
        out_specs=[vmem] * (1 + len(widths)),
        out_shape=[jax.ShapeDtypeStruct((joined, features), BF16)]
        + [jax.ShapeDtypeStruct((depth, width), BF16) for width in widths],
        compiler_params=params(58),
        cost_estimate=cost(),
    )(prefix, latent_in, w_self_qkv, w_self_out, w_gate_up, w_down)


def start_copies(rows_ref, out_refs, sems):
    depth = rows_ref.shape[3]
    x = lax.axis_index("x")
    first = 0
    for n, out_ref in enumerate(out_refs):
        columns = pl.ds(first, out_ref.shape[1])
        first += out_ref.shape[1]
        for z in range(DEPTH):
            for core in range(CORES):
                for k in range(BREADTH):
                    chip = z * BREADTH + behind(x, k, BREADTH)
                    at = pl.multiple_of((chip * CORES + core) * depth, depth)
                    pltpu.make_async_copy(
                        rows_ref.at[z, core, k, :, columns],
                        out_ref.at[pl.ds(at, depth)],
                        sems.at[n],
                    ).start()


def wait_copies(out_ref, sem):
    pltpu.make_async_copy(out_ref, out_ref, sem).wait()


def assemble(rows, splits):
    def body(rows_ref, *refs):
        out_refs, sems = refs[:-1], refs[-1]
        start_copies(rows_ref, out_refs, sems)
        for n, out_ref in enumerate(out_refs):
            wait_copies(out_ref, sems.at[n])

    count = DEPTH * BREADTH * CORES * rows.shape[3]
    return pl.pallas_call(
        body,
        in_specs=[pl.BlockSpec(memory_space=pl.ANY)],
        out_specs=[pl.BlockSpec(memory_space=pltpu.VMEM)] * len(splits),
        out_shape=[jax.ShapeDtypeStruct((count, width), BF16) for width in splits],
        scratch_shapes=[pltpu.SemaphoreType.DMA((len(splits),))],
        compiler_params=params(58),
        cost_estimate=cost(),
    )(rows)


def project_head(normed, weight):
    rows, width = normed[0].shape

    def body(*refs):
        latents = jnp.concatenate([ref[...] for ref in refs[:BREADTH]], axis=0)
        weight_ref, query_ref, keyval_ref = refs[BREADTH:]
        out = jnp.dot(latents, weight_ref[...], preferred_element_type=F32).astype(BF16)
        query_ref[...] = out[:, :HD]
        for z in range(DEPTH):
            keyval_ref[z] = out[:, HD:]

    whole = lambda *shape: pl.BlockSpec(shape, lambda i: (0, 0))
    return pl.pallas_call(
        body,
        grid=(1,),
        in_specs=[whole(rows, width)] * BREADTH + [whole(width, 3 * HD)],
        out_specs=[
            whole(BREADTH * rows, HD),
            pl.BlockSpec((DEPTH, BREADTH * rows, 2 * HD), lambda i: (0, 0, 0)),
        ],
        out_shape=[
            jax.ShapeDtypeStruct((BREADTH * rows, HD), BF16),
            jax.ShapeDtypeStruct((DEPTH, BREADTH * rows, 2 * HD), BF16),
        ],
        compiler_params=params(48),
        cost_estimate=cost(),
    )(*normed, weight)


def self_attention(rows, queries, mine, other, weight):
    total_rows, width = queries.shape
    count = mine.shape[0]
    features = weight.shape[0]

    def index(n, x, core):
        at_z, at_x = n // total_rows, (x + BREADTH - (n // rows) % BREADTH) % BREADTH
        return ((at_z * BREADTH + at_x) * CORES + core) * rows + n % rows

    def body(q_ref, mine_ref, other_ref, weight_ref, *out_refs):
        z, x, core = [lax.axis_index(name) for name in SEQ]
        n = lax.broadcasted_iota(jnp.int32, (1, count), 1)
        key = index(n, x, core)
        keys = (key, key + (1 - 2 * core) * rows)
        n = z * total_rows + lax.broadcasted_iota(jnp.int32, (total_rows, 1), 0)
        row = index(n, x, core)
        found = []
        for ref, key in zip((mine_ref, other_ref), keys):
            s = lax.dot_general(q_ref[...], ref[:, :width], NT, preferred_element_type=F32)
            found.append(jnp.where(key <= row, s * SCALE, NEG))
        peak = jnp.maximum(*[jnp.max(s, axis=1, keepdims=True) for s in found])
        total = jnp.zeros_like(peak)
        summed = jnp.zeros((total_rows, width), F32)
        for s, ref in zip(found, (mine_ref, other_ref)):
            weights = jnp.exp(s - peak)
            total = total + jnp.sum(weights, axis=1, keepdims=True)
            for part in split(weights):
                summed = summed + jnp.dot(part, ref[:, width:], preferred_element_type=F32)
        context = (summed / total).astype(BF16)
        out = lax.dot_general(context, weight_ref[...], NT, preferred_element_type=F32)
        out = out.astype(BF16)
        for k, ref in enumerate(out_refs):
            ref[...] = out[k * rows : (k + 1) * rows]

    return pl.pallas_call(
        body,
        out_shape=[jax.ShapeDtypeStruct((rows, features), BF16)] * BREADTH,
        compiler_params=params(48),
        cost_estimate=cost(),
    )(queries, mine, other, weight)


def norm_own(base, terms, gain):
    rows, width = base.shape
    piece = width // TP

    def body(base_ref, a, b, c, d, gain_ref, own_ref, normed_ref, total_ref):
        tp = lax.axis_index("tp")
        total, normed = add_and_norm(base_ref, (a, b, c, d), gain_ref)
        total_ref[...] = total
        normed_ref[...] = normed
        own_ref[...] = total_ref[:, pl.ds(pl.multiple_of(tp * piece, piece), piece)]

    vmem = pl.BlockSpec(memory_space=pltpu.VMEM)
    return pl.pallas_call(
        body,
        in_specs=[vmem] * 6,
        out_specs=[vmem] * 2,
        out_shape=[
            jax.ShapeDtypeStruct((rows, piece), BF16),
            jax.ShapeDtypeStruct((rows, width), BF16),
        ],
        scratch_shapes=[pltpu.VMEM((rows, width), BF16)],
        compiler_params=params(),
        cost_estimate=cost(),
    )(base, *terms, gain)


def mlp(normed, weight):
    rows, width = normed[0].shape
    share = weight.shape[-1] // 3
    piece = width // TP

    def body(*refs):
        rows_ref, out_ref, both_ref, down_ref, sems = refs[BREADTH:]
        x = lax.axis_index("x")
        start_copies(rows_ref, (both_ref, down_ref), sems)
        latents = jnp.concatenate([ref[...] for ref in refs[:BREADTH]], axis=0)
        wait_copies(both_ref, sems.at[0])
        both = jnp.dot(latents, both_ref[...], preferred_element_type=F32)
        inner = (jax.nn.silu(both[:, :share]) * both[:, share:]).astype(BF16)
        wait_copies(down_ref, sems.at[1])
        for t in range(TP):
            term = lax.dot_general(
                inner,
                down_ref[t * piece : (t + 1) * piece, :],
                NT,
                preferred_element_type=F32,
            ).astype(BF16)
            for k in range(BREADTH):
                out_ref[behind(x, k, BREADTH) * TP + t] = term[k * rows : (k + 1) * rows]

    vmem = pl.BlockSpec(memory_space=pltpu.VMEM)
    return pl.pallas_call(
        body,
        in_specs=[vmem] * BREADTH
        + [pl.BlockSpec(memory_space=pl.ANY)],
        out_specs=vmem,
        out_shape=jax.ShapeDtypeStruct((BREADTH * TP, rows, piece), BF16),
        scratch_shapes=[
            pltpu.VMEM((width, 2 * share), BF16),
            pltpu.VMEM((width, share), BF16),
            pltpu.SemaphoreType.DMA((2,)),
        ],
        compiler_params=params(32),
        cost_estimate=cost(),
    )(*normed, weight)


def local(
    prefix,
    latent_in,
    latent_pos,
    w_query,
    w_keyval,
    w_cross_out,
    attn_gain,
    w_self_qkv,
    w_self_out,
    mlp_gain,
    w_gate_up,
    w_down,
):
    chips = lax.axis_size(ZX)
    core = lax.axis_index("core")
    rows = latent_in.shape[0]
    joined, *heads = pack(prefix, latent_in, w_self_qkv, w_self_out.T, w_gate_up, w_down.T)
    pieces = everyone(joined)
    positions = prefix.shape[0]
    beside = [shifted(heads[k + 1], "x", k, BREADTH) for k in range(1, BREADTH)]
    head_rows = jnp.stack([heads[0]] + [piece[:, : 4 * HD] for piece in beside])
    unit_rows = jnp.stack([heads[1]] + [piece[:, 4 * HD :] for piece in beside])

    pieces, head_rows = lax.optimization_barrier((pieces, head_rows))
    queries, latents, *keyval = project_gathered(pieces, positions, w_query, w_keyval)
    all_queries = lax.all_to_all(queries, ZX, 0, 0).reshape(chips * rows, HD)
    head_rows = lax.all_gather(head_rows, ("z", "core"), axis=0)

    keyval = [keyval[0]] + [shifted(keyval[k], "x", k, BREADTH) for k in range(1, BREADTH)]
    keyval = keyval + [shifted(piece, "core", 1, CORES) for piece in keyval]
    pos = lax.dynamic_index_in_dim(
        latent_pos.reshape(chips, CORES, rows), core, axis=1, keepdims=False
    ).reshape(1, chips * rows)
    partial = cross_partial(pos, all_queries, keyval)
    partial = lax.all_to_all(partial.reshape(chips, rows, -1), ZX, 0, 0)
    partial = partial.reshape(DEPTH, BREADTH, rows, -1)
    split_cores = lambda x: x.reshape(DEPTH, CORES, *x.shape[1:])
    weights = assemble(split_cores(head_rows), (3 * HD, HD))
    partial, weights, unit_rows = lax.optimization_barrier((partial, weights, unit_rows))
    unit_rows = lax.all_gather(unit_rows, ("z", "core"), axis=0)
    w_qkv, w_out = weights
    cross_terms = combine_and_project(partial, w_cross_out)

    first, normed = norm(latents, everyone(cross_terms), attn_gain[None])
    group = [normed] + [shifted(normed, "x", k, BREADTH) for k in range(1, BREADTH)]
    queries, keyval = project_head(group, w_qkv)
    mine = lax.all_to_all(keyval, "z", 0, 0).reshape(-1, keyval.shape[2])
    other = shifted(mine, "core", 1, CORES)
    terms = self_attention(rows, queries, mine, other, w_out)
    terms = [terms[0]] + [shifted(terms[k], "x", BREADTH - k, BREADTH) for k in range(1, BREADTH)]
    out_terms = sum(term.astype(F32) for term in terms).astype(BF16)

    own, normed = norm_own(first, everyone(out_terms), mlp_gain[None])
    group = [normed] + [shifted(normed, "x", k, BREADTH) for k in range(1, BREADTH)]
    down_terms = lax.all_to_all(mlp(group, split_cores(unit_rows)), ("x", "tp"), 0, 0)
    return (own.astype(F32) + jnp.sum(down_terms.astype(F32), axis=0)).astype(BF16)


def solution(mesh):
    z, x, core, y = DEPTH, BREADTH, CORES, TP
    grid = Mesh(mesh.devices.reshape(z, x, core, y), ("z", "x", "core", "tp"))
    return jax.shard_map(
        local,
        mesh=grid,
        in_specs=(
            P(SEQ, "tp"),
            P(SEQ, "tp"),
            P(),
            P(None, "tp"),
            P(None, None, "tp"),
            P("tp", None),
            P(),
            P(None, SEQ, "tp"),
            P("tp", SEQ),
            P(),
            P(None, SEQ, "tp"),
            P("tp", SEQ),
        ),
        out_specs=P(SEQ, "tp"),
        check_vma=False,
    )
```
